768 devices in a mesh: rep: 12 (over x, z_lo), fsdp: 64 (over y, z_hi, core).
Axes of the slice: x: 4, y: 8, z: 12 (z_hi: 4, z_lo: 3; z = z_hi * 3 + z_lo), core: 2. Of those that a mesh axis runs over, the one named last changes fastest.
Arguments:
- activations: bfloat16 [98304, 8192], P(('rep', 'fsdp')), may hold values from -54 to 54, as said below
- out_grad: bfloat16 [98304, 128], P(('rep', 'fsdp')), may hold values from -12 to 12
- key_weight: bfloat16 [8192, 128], P('fsdp'), may hold values from -0.0625 to 0.0625
- lengths: int32 [768, 8], P(('rep', 'fsdp')), may hold values from 0 to 128, as said below
Outputs:
- grad_in: bfloat16 [98304, 8192], P(('rep', 'fsdp'))
- weight_grad: float32 [8192, 128], P('fsdp')
- factor: float32 [1024, 1024], P('fsdp')
The draws below stay inside these ranges and needn't reach their ends.
Inputs may be any that keep to these rules, and one draw needn't show every extreme that they name: Row d lists, in order, the lengths of the sequences packed from the start of device d's 128 token slots, zero for unused entries; slots past a row's sum are padding. Each row sums to between 1 and 128; the last row holds one sequence of exactly 128 and zeros. `activations`: activations are finite and within the stated range.
All inputs are finite; a program needn't handle non-finite values.
Results may differ from the reference program's by a relative error of at most 0.0015.
Values may be sent and summed in bfloat16 or wider, within the bound.
A program may use at most 64 MiB of HBM per device.

```python
import math
import jax
import jax.numpy as jnp
from jax import lax

FEATURES = 8192
HEAD = 128
FBLK = 1024
SLOTS = 8
TOK_DEV = 128
SHARDS = 768
TOKENS = 98304


def draw_activations(key, part):
    key = jax.random.fold_in(key, 5)
    key_base, key_rows, key_cols = jax.random.split(key, 3)
    base = jnp.clip(jax.random.normal(key_base, (TOKENS, FEATURES), jnp.float32), -6.0, 6.0)
    rows = jnp.exp(jax.random.uniform(key_rows, (TOKENS, 1), jnp.float32, math.log(0.3), math.log(3.0)))
    cols = jnp.exp(jax.random.uniform(key_cols, (1, FEATURES), jnp.float32, math.log(0.3), math.log(3.0)))
    return (base * rows * cols).astype(jnp.bfloat16)


def draw_lengths(key, part):
    key = jax.random.fold_in(key, 11)
    key_jitter, key_cuts = jax.random.split(key, 2)
    index = jnp.arange(SHARDS, dtype=jnp.int32)
    lowest = TOK_DEV // 16
    denom = max((SHARDS - 1) * (SHARDS - 1), 1)
    ramp = lowest + index * index * (TOK_DEV - lowest) // denom
    jitter = jax.random.randint(key_jitter, (SHARDS,), 0, max(TOK_DEV // 16, 1), dtype=jnp.int32)
    valid = jnp.clip(ramp - jitter, 1, TOK_DEV)
    last_row = index == SHARDS - 1
    valid = jnp.where(last_row, TOK_DEV, valid).astype(jnp.int32)
    cuts = jax.random.randint(key_cuts, (SHARDS, SLOTS - 1), 1, TOK_DEV, dtype=jnp.int32)
    cuts = jnp.where(last_row[:, None], valid[:, None], cuts)
    cuts = jnp.sort(jnp.minimum(cuts, valid[:, None]), axis=1)
    bounds = jnp.concatenate([jnp.zeros((SHARDS, 1), jnp.int32), cuts, valid[:, None]], axis=1)
    return (bounds[:, 1:] - bounds[:, :-1]).astype(jnp.int32)


def levels(rng, dims, cuts, smallest, top_value):
    def one(dim, blocks):
        heights = jax.random.uniform(jax.random.fold_in(jax.random.fold_in(rng, 6), dim), (blocks,), jnp.float32, smallest / len(cuts), top_value / len(cuts))
        return jnp.repeat(jnp.exp(heights), dims[dim] // blocks).reshape((-1,) + (1,) * (len(dims) - dim - 1))

    level = one(*cuts[0])
    for cut in cuts[1:]:
        level = level * one(*cut)
    return level


def bell_draw(rng, dims, deviation, most, pieces=(), held_as=jnp.bfloat16):
    result = jax.random.normal(rng, dims, jnp.float32) * deviation
    if len(pieces) > 0:
        result = levels(rng, dims, pieces, -0.22, 0.18) * result
    return jnp.clip(result, min=-most, max=most).astype(held_as)


def setup_inputs(seed: int = 0) -> dict:
    key_of = jax.random.split(jax.random.key(seed), 5)
    return {
        "activations": draw_activations(jax.random.fold_in(key_of[4], 71), 0),
        "out_grad": bell_draw(key_of[1], (TOKENS, HEAD), 2.0, 12.0, ((0, 768),)),
        "key_weight": bell_draw(key_of[2], (FEATURES, HEAD), FEATURES ** -0.5, 0.0625, ((0, 64),)),
        "lengths": draw_lengths(jax.random.fold_in(key_of[4], 71), 0),
    }


def reference(activations, out_grad, key_weight, lengths):
    ends = jnp.cumsum(lengths, axis=1)
    starts = ends - lengths
    position = jnp.arange(TOK_DEV, dtype=jnp.int32)[None, :, None]
    member = (position >= starts[:, None, :]) & (position < ends[:, None, :])
    inverse = 1.0 / jnp.maximum(lengths, 1).astype(jnp.float32)
    ratio = jnp.sum(jnp.where(member, inverse[:, None, :], jnp.float32(0.0)), axis=2).reshape(TOKENS)
    total_valid = jnp.sum(lengths).astype(jnp.float32)
    total_seqs = jnp.sum((lengths > 0).astype(jnp.float32))
    scale = total_valid / total_seqs
    scaled_grad = (out_grad.astype(jnp.float32) * ratio[:, None]).astype(jnp.bfloat16)
    grouped = scaled_grad.reshape(SHARDS, TOK_DEV, HEAD)

    def one_device(rows):
        product = lax.dot_general(rows, key_weight, (((1,), (1,)), ((), ())), preferred_element_type=jnp.float32)
        return (scale * product).astype(jnp.bfloat16)

    grad_in = lax.map(one_device, grouped).reshape(TOKENS, FEATURES)
    weight_grad = scale * lax.dot_general(activations, scaled_grad, (((0,), (0,)), ((), ())), preferred_element_type=jnp.float32)
    block = activations[:, :FBLK]
    weighted_block = (block.astype(jnp.float32) * ratio[:, None]).astype(jnp.bfloat16)
    gram = lax.dot_general(block, weighted_block, (((0,), (0,)), ((), ())), preferred_element_type=jnp.float32)
    return grad_in, weight_grad, gram / total_seqs
```

```python
import jax
import jax.numpy as jnp
from jax import lax
from jax.experimental import pallas as pl
from jax.experimental.pallas import tpu as pltpu
from jax.sharding import PartitionSpec as P

FBLK = 1024
X, Y, ZH, ZL = 4, 8, 4, 3
Z = ZH * ZL
T = 128
MESH = pl.DeviceIdType.MESH
F32, BF16 = jnp.float32, jnp.bfloat16


def ratio_of(tile):
    pos = lax.broadcasted_iota(jnp.int32, (T, T), 0)
    end = jnp.zeros((1, T), jnp.int32)
    ratio = jnp.zeros((T, T), F32)
    for s in range(8):
        length = tile[s:s + 1, :]
        start, end = end, end + length
        inverse = 1.0 / jnp.maximum(length, 1).astype(F32)
        ratio = ratio + jnp.where((pos >= start) & (pos < end), inverse, 0.0)
    return ratio


def kernel(
    act, og, kw, lens, grad_in, wgrad, factor,
    abuf, sgt, sgs, psum, xr, ybuf, yr, yl, gblk, wbt, lt, cy, cz,
    wbuf, gbuf, zbuf, zr, lr, finw, finf, fw, ff, ogv, ss, rs, ls,
):
    rep, fs = lax.axis_index("rep"), lax.axis_index("fsdp")
    x, zl = lax.div(rep, ZL), lax.rem(rep, ZL)
    y, zh, c = lax.div(fs, 8), lax.rem(lax.div(fs, 2), ZH), lax.rem(fs, 2)
    z = zh * ZL + zl

    def dev(dx=0, dy=0, dz=0, dc=0, dzh=0, dzl=0):
        x2, y2 = lax.rem(x + dx, X), lax.rem(y + dy, Y)
        if dz:
            z2 = lax.rem(z + dz, Z)
            zh2, zl2 = lax.div(z2, ZL), lax.rem(z2, ZL)
        else:
            zh2, zl2 = lax.rem(zh + dzh, ZH), lax.rem(zl + dzl, ZL)
        c2 = 1 - c if dc else c
        return (x2 * ZL + zl2, y2 * 8 + zh2 * 2 + c2)

    sib, right, left = dev(dc=1), dev(dx=1), dev(dx=3)
    up, down = dev(dy=1), dev(dy=7)
    group = [right, left, dev(dx=2), sib, dev(dx=1, dc=1), dev(dx=3, dc=1), dev(dx=2, dc=1)]
    count = [0]
    sent = []

    def send(src, dst, to):
        k = count[0]
        count[0] += 1
        copy = pltpu.make_async_remote_copy(
            src_ref=src, dst_ref=dst, send_sem=ss.at[k], recv_sem=rs.at[k],
            device_id=to, device_id_type=MESH,
        )
        copy.start()
        sent.append(copy)
        return copy

    def cols(b):
        return act.at[:, pl.ds(pl.multiple_of(b * T, T), T)]

    def start_own(i, _):
        pltpu.make_async_copy(cols(2 * i + c), abuf.at[i, 0], ls.at[0]).start()
        return 0

    lax.fori_loop(0, 32, start_own, 0)
    own_all = pltpu.make_async_copy(abuf.at[:, 0], abuf.at[:, 0], ls.at[0])
    og_copy = pltpu.make_async_copy(og, ogv, ls.at[1])
    og_copy.start()
    w_copy = pltpu.make_async_copy(kw, wbuf.at[y, zh, c], ls.at[2])
    w_copy.start()
    blk_copy = pltpu.make_async_copy(act.at[:, 0:FBLK], gblk.at[0], ls.at[3])
    blk_copy.start()

    barrier = pltpu.get_barrier_semaphore()
    peers = group + [dev(dy=d) for d in range(1, Y)] + [dev(dz=d) for d in range(1, Z)]
    for peer in peers:
        pl.semaphore_signal(barrier, inc=1, device_id=peer, device_id_type=MESH)
    pl.semaphore_wait(barrier, len(peers))

    g_r = send(act.at[:, 0:FBLK], gblk.at[1], right)
    g_l = send(act.at[:, 0:FBLK], gblk.at[2], left)
    act_k = count[0]
    count[0] += 2

    def swap(half):
        k = act_k + half

        def start(i, _):
            pltpu.make_async_remote_copy(
                src_ref=cols(2 * i + 1 - c), dst_ref=abuf.at[i, 1], send_sem=ss.at[k], recv_sem=rs.at[k],
                device_id=sib, device_id_type=MESH,
            ).start()
            return 0

        lax.fori_loop(16 * half, 16 * half + 16, start, 0)
        part = abuf.at[16 * half:16 * half + 16]
        whole = pltpu.make_async_remote_copy(
            src_ref=part.at[:, 0], dst_ref=part.at[:, 1], send_sem=ss.at[k], recv_sem=rs.at[k],
            device_id=sib, device_id_type=MESH,
        )
        sent.append(whole)
        return whole

    swap_a, swap_b = swap(0), swap(1)
    w_zh = [send(kw, wbuf.at[y, zh, c], dev(dzh=d)) for d in range(1, ZH)]

    row = lax.broadcasted_iota(jnp.int32, (8, T), 0)
    tile = jnp.zeros((8, T), jnp.int32)
    for s in range(8):
        tile = jnp.where(row == s, lens[0, s], tile)
    lt[0] = tile
    l_copies = [send(lt.at[0], lt.at[1 + i], to) for i, to in enumerate(group)]
    og_copy.wait()
    scaled = ogv[...].astype(F32) * ratio_of(tile)
    sgs[...] = scaled.astype(BF16)
    sgt[0] = scaled.T.astype(BF16)
    s_copy = send(sgt.at[0], sgt.at[1], sib)
    blk_copy.wait()
    g_s = [send(gblk.at[0], gblk.at[4], sib)]

    own_all.wait()
    s_copy.wait_recv()
    heads = jnp.concatenate([sgt[0], sgt[1]], axis=1)

    def weight_block(i, _):
        out = jnp.dot(heads, abuf[i].reshape(2 * T, T), preferred_element_type=F32)
        psum[:, i] = out.reshape(X, 32, T)
        return 0

    xp, xm, xo = lax.rem(x + 1, X), lax.rem(x + 3, X), lax.rem(x + 2, X)
    swap_a.wait_recv()
    lax.fori_loop(0, 16, weight_block, 0)
    r1 = send(psum.at[xo, 0:16], xr.at[0], right)
    l2 = None
    swap_b.wait_recv()
    lax.fori_loop(16, 32, weight_block, 0)
    l1 = send(psum.at[xo, 16:32], xr.at[1], left)
    r2 = send(psum.at[xp, 16:32], xr.at[2], right)
    l2 = send(psum.at[xm, 0:16], xr.at[3], left)

    w_copy.wait()
    for copy in w_zh:
        copy.wait_recv()

    def w_step(s):
        lo, hi = lax.rem(y + Y - s, Y), lax.rem(y + s, Y)
        if s < 3:
            return [
                send(wbuf.at[lo, :, c], wbuf.at[lo, :, c], up),
                send(wbuf.at[hi, :, c], wbuf.at[hi, :, c], down),
            ]
        return [
            send(wbuf.at[lo, 0:2, c], wbuf.at[lo, 0:2, c], up),
            send(wbuf.at[hi, 2:4, c], wbuf.at[hi, 2:4, c], down),
        ]

    def arrived(copies):
        for copy in copies:
            copy.wait_recv()

    w_now = w_step(0)

    arrived(l_copies)
    every = lt[...]
    cy[0, 0:8] = jnp.sum(every, axis=0).astype(F32)
    cy[0, 8:16] = jnp.sum((every > 0).astype(jnp.int32), axis=0).astype(F32)
    y_counts = [send(cy.at[0], cy.at[d], dev(dy=d)) for d in range(1, Y)]

    g_r.wait_recv()
    f_r = send(gblk.at[1, 0:64], gblk.at[3, 0:64], right)
    g_l.wait_recv()
    f_l = send(gblk.at[2, 64:128], gblk.at[3, 64:128], left)
    g_s.append(send(gblk.at[1], gblk.at[5], sib))
    g_s.append(send(gblk.at[2], gblk.at[6], sib))

    arrived(y_counts)
    cz[0] = jnp.sum(cy[...], axis=0)
    z_counts = [send(cz.at[0], cz.at[d], dev(dz=d)) for d in range(1, Z)]

    arrived(w_now)
    w_now = w_step(1)

    r1.wait_recv()
    psum[xp, 0:16] += xr[0]
    r3 = send(psum.at[xp, 0:16], xr.at[4], right)
    l1.wait_recv()
    psum[xm, 16:32] += xr[1]
    l3 = send(psum.at[xm, 16:32], xr.at[5], left)

    arrived(w_now)
    w_now = w_step(2)

    arrived([f_r, f_l])
    g_s.append(send(gblk.at[3], gblk.at[7], sib))
    mine = pl.ds(pl.multiple_of((2 * x + c) * T, T), T)

    def weigh(s):
        weighted = gblk[s, :, mine].astype(F32) * ratio_of(lt[s])
        wbt[:, s * T:(s + 1) * T] = weighted.T.astype(BF16)

    for s in range(4):
        weigh(s)
    for s in range(4):
        g_s[s].wait_recv()
        weigh(4 + s)

    def factor_block(i, _):
        part = gblk[:, :, pl.ds(pl.multiple_of(i * T, T), T)].reshape(8 * T, T)
        ybuf[1, i] = jnp.dot(wbt[...], part, preferred_element_type=F32)
        return 0

    lax.fori_loop(0, Y, factor_block, 0)

    def y_step(p, s, before):
        t = 4 - s
        hi, lo = lax.rem(y + t, Y), lax.rem(y + Y - t, Y)
        if s == 0:
            return [
                send(ybuf.at[p, hi, 0:64], yr.at[p, 0, 0:64], up),
                send(ybuf.at[p, hi, 64:128], yl.at[p, 0, 64:128], down),
            ]
        before[0].wait_recv()
        if s == 1:
            ybuf[p, hi, 0:64] += yr[p, 0, 0:64]
        else:
            ybuf[p, hi] += yr[p, s - 1]
        a = send(ybuf.at[p, hi], yr.at[p, s], up)
        before[1].wait_recv()
        if s == 1:
            ybuf[p, lo, 64:128] += yl[p, 0, 64:128]
        else:
            ybuf[p, lo] += yl[p, s - 1]
        b = send(ybuf.at[p, lo], yl.at[p, s], down)
        return [a, b]

    f_y = y_step(1, 0, None)
    arrived(w_now)
    w_now = w_step(3)
    f_y = y_step(1, 1, f_y)

    l2.wait_recv()
    r3.wait_recv()
    ybuf[0, 0:4] = (psum[x, 0:16] + xr[3] + xr[4]).reshape(4, T, T)
    r2.wait_recv()
    l3.wait_recv()
    ybuf[0, 4:8] = (psum[x, 16:32] + xr[2] + xr[5]).reshape(4, T, T)
    g_y = y_step(0, 0, None)
    f_y = y_step(1, 2, f_y)
    arrived(w_now)
    w_swap = send(wbuf.at[:, :, c], wbuf.at[:, :, c], sib)
    g_y = y_step(0, 1, g_y)
    f_y = y_step(1, 3, f_y)

    arrived(z_counts)
    total = jnp.sum(cz[...], axis=0)
    valid = jnp.sum(total[0:8], axis=0, keepdims=True)
    seqs = jnp.sum(total[8:16], axis=0, keepdims=True)
    scale_row = valid / seqs
    scale = jnp.max(scale_row)

    g_y = y_step(0, 2, g_y)
    w_swap.wait_recv()

    def product(i):
        out = lax.dot_general(
            sgs[...], wbuf[i].reshape(1024, T), (((1,), (1,)), ((), ())), preferred_element_type=F32
        )
        gbuf[:, i * 1024:(i + 1) * 1024] = (scale * out).astype(BF16)

    for i in range(4):
        product(i)
    arrived(f_y)
    turned = (ybuf[1, y] + yr[1, 3] + yl[1, 3]).T
    zbuf[:, 32:64] = turned.reshape(ZH, 32, T)
    g_y = y_step(0, 3, g_y)
    for i in range(4, 8):
        product(i)
    out_copy = pltpu.make_async_copy(gbuf, grad_in, ls.at[4])
    out_copy.start()
    arrived(g_y)
    zbuf[:, 0:32] = (ybuf[0, y] + yr[0, 3] + yl[0, 3]).reshape(ZH, 32, T)

    z_copies = [send(zbuf.at[lax.rem(zh + d, ZH)], zr.at[d], dev(dzh=d)) for d in range(1, ZH)]
    zr[0] = zbuf[zh]
    arrived(z_copies)
    lr[0] = zr[0] + zr[1] + zr[2] + zr[3]
    l_sums = [send(lr.at[0], lr.at[d], dev(dzl=d)) for d in range(1, ZL)]
    arrived(l_sums)
    done = lr[0] + lr[1] + lr[2]
    finw[...] = done[0:32]
    finf[...] = done[32:64].reshape(2, 16, T)
    slot = 2 * x + c
    last = [send(finw, fw.at[x], to) for to in group[:3]]
    last += [send(finf.at[c], ff.at[slot], to) for to in group[:3]]
    last += [send(finf.at[1 - c], ff.at[slot], to) for to in group[3:]]
    fw[x] = done[0:32]
    ff[slot] = finf[c]
    arrived(last)
    wgrad[...] = scale * fw[...].reshape(T, T).T
    for g in range(8):
        factor[:, g * T:(g + 1) * T] = ff[g] / seqs
    out_copy.wait()
    for copy in sent:
        copy.wait_send()


def shards(activations, out_grad, key_weight, lengths):
    sems = 160
    any_space = pl.BlockSpec(memory_space=pl.ANY)
    vmem = pl.BlockSpec(memory_space=pltpu.VMEM)
    return pl.pallas_call(
        kernel,
        out_shape=(
            jax.ShapeDtypeStruct((T, 8192), BF16),
            jax.ShapeDtypeStruct((T, T), F32),
            jax.ShapeDtypeStruct((16, FBLK), F32),
        ),
        in_specs=[any_space, any_space, any_space, pl.BlockSpec(memory_space=pltpu.SMEM)],
        out_specs=(any_space, vmem, vmem),
        scratch_shapes=[
            pltpu.VMEM((32, 2, T, T), BF16),
            pltpu.VMEM((2, T, T), BF16),
            pltpu.VMEM((T, T), BF16),
            pltpu.VMEM((X, 32, 32, T), F32),
            pltpu.VMEM((6, 16, 32, T), F32),
            pltpu.VMEM((2, Y, T, T), F32),
            pltpu.VMEM((2, 4, T, T), F32),
            pltpu.VMEM((2, 4, T, T), F32),
            pltpu.VMEM((8, T, FBLK), BF16),
            pltpu.VMEM((T, 8 * T), BF16),
            pltpu.VMEM((8, 8, T), jnp.int32),
            pltpu.VMEM((Y, 16, T), F32),
            pltpu.VMEM((Z, 16, T), F32),
            pltpu.VMEM((Y, ZH, 2, T, T), BF16),
            pltpu.VMEM((T, 8192), BF16),
            pltpu.VMEM((ZH, 64, T), F32),
            pltpu.VMEM((ZH, 64, T), F32),
            pltpu.VMEM((ZL, 64, T), F32),
            pltpu.VMEM((32, T), F32),
            pltpu.VMEM((2, 16, T), F32),
            pltpu.VMEM((X, 32, T), F32),
            pltpu.VMEM((8, 16, T), F32),
            pltpu.VMEM((T, T), BF16),
            pltpu.SemaphoreType.DMA((sems,)),
            pltpu.SemaphoreType.DMA((sems,)),
            pltpu.SemaphoreType.DMA((8,)),
        ],
        compiler_params=pltpu.CompilerParams(
            collective_id=0, has_side_effects=True, vmem_limit_bytes=48 * 1024 * 1024
        ),
    )(activations, out_grad, key_weight, lengths)


def solution(mesh):
    in_specs = (
        P(("rep", "fsdp"), None),
        P(("rep", "fsdp"), None),
        P("fsdp", None),
        P(("rep", "fsdp"), None),
    )
    out_specs = (P(("rep", "fsdp"), None), P("fsdp", None), P("fsdp", None))
    return jax.shard_map(shards, mesh=mesh, in_specs=in_specs, out_specs=out_specs, check_vma=False)
```

```python
import jax
import jax.numpy as jnp
from jax import lax
from jax.experimental import pallas as pl
from jax.experimental.pallas import tpu as pltpu
from jax.sharding import PartitionSpec as P

FBLK = 1024
X, Y, ZH, ZL = 4, 8, 4, 3
T = 128
MESH = pl.DeviceIdType.MESH
F32, BF16 = jnp.float32, jnp.bfloat16


def ratio_of(tile):
    pos = lax.broadcasted_iota(jnp.int32, (T, T), 0)
    end = jnp.zeros((1, T), jnp.int32)
    ratio = jnp.zeros((T, T), F32)
    for s in range(8):
        length = tile[s:s + 1, :]
        start, end = end, end + length
        inverse = 1.0 / jnp.maximum(length, 1).astype(F32)
        ratio = ratio + jnp.where((pos >= start) & (pos < end), inverse, 0.0)
    return ratio


def kernel(
    act, og, kw, lens, grad_in, wgrad, factor,
    abuf, sgt, sgs, psum, xr, yb, ybr, ybl, ya, yar, yal, yf, yfr, yfl, xb, xbr, gblk, wbt, lt, cy, cz, cl,
    wbuf, zw, zwr, zf, zfr, lr, finw, finf, fw, ff, ogv, lens_s, ss, rs, ls,
):
    rep, fs = lax.axis_index("rep"), lax.axis_index("fsdp")
    x, zl = lax.div(rep, ZL), lax.rem(rep, ZL)
    y, zh, c = lax.div(fs, 8), lax.rem(lax.div(fs, 2), ZH), lax.rem(fs, 2)

    def dev(dx=0, dy=0, dzh=0, dzl=0, dc=0):
        c2 = 1 - c if dc else c
        x2, y2, zh2, zl2 = lax.rem(x + dx, X), lax.rem(y + dy, Y), lax.rem(zh + dzh, ZH), lax.rem(zl + dzl, ZL)
        return (x2 * ZL + zl2, y2 * 8 + zh2 * 2 + c2)

    sib, right, left = dev(dc=1), dev(dx=1), dev(dx=3)
    up, down = dev(dy=1), dev(dy=7)
    fore, back = dev(dzh=1), dev(dzh=3)
    group = [right, left, sib, dev(dx=1, dc=1), dev(dx=3, dc=1), dev(dx=2), dev(dx=2, dc=1)]
    same, other = [group[0], group[1], group[5]], [group[2], group[3], group[4], group[6]]
    ys = [dev(dy=d) for d in range(1, Y)]
    zhs = [dev(dzh=d) for d in range(1, ZH)]
    zls = [dev(dzl=d) for d in range(1, ZL)]
    count = [0]
    sent = []

    def send(src, dst, to):
        k = count[0]
        count[0] += 1
        copy = pltpu.make_async_remote_copy(
            src_ref=src, dst_ref=dst, send_sem=ss.at[k], recv_sem=rs.at[k],
            device_id=to, device_id_type=MESH,
        )
        copy.start()
        sent.append(copy)
        return copy

    def arrived(copies):
        for copy in copies:
            copy.wait_recv()

    lens_copy = pltpu.make_async_copy(lens, lens_s, ls.at[4])
    lens_copy.start()
    og_copy = pltpu.make_async_copy(og, ogv, ls.at[1])
    og_copy.start()

    barrier = pltpu.get_barrier_semaphore()
    peers = group + ys + zhs + zls
    for peer in peers:
        pl.semaphore_signal(barrier, inc=1, device_id=peer, device_id_type=MESH)

    def cols(i, half, core):
        b = lax.div(i, 2) * 8 + half * 4 + lax.rem(i, 2) * 2 + core
        return act.at[:, pl.ds(pl.multiple_of(b * T, T), T)]

    for half in range(2):
        def start_own(i, _, half=half):
            pltpu.make_async_copy(cols(i, half, c), abuf.at[16 * half + i, 0], ls.at[0]).start()
            return 0

        lax.fori_loop(0, 16, start_own, 0)
    own_all = pltpu.make_async_copy(abuf.at[:, 0], abuf.at[:, 0], ls.at[0])
    blk_copy = pltpu.make_async_copy(act.at[:, 0:FBLK], gblk.at[0], ls.at[3])
    blk_copy.start()
    part = pl.ds(pl.multiple_of(32 * x, 32), 32)
    w_copy = pltpu.make_async_copy(kw.at[part], wbuf.at[y, zh, c, part], ls.at[2])
    w_copy.start()

    lens_copy.wait()
    row = lax.broadcasted_iota(jnp.int32, (8, T), 0)
    tile = jnp.zeros((8, T), jnp.int32)
    for s in range(8):
        tile = jnp.where(row == s, lens_s[0, s], tile)
    lt[0] = tile
    og_copy.wait()
    scaled = ogv[...].astype(F32) * ratio_of(tile)
    sgs[...] = scaled.astype(BF16)
    sgt[0] = scaled.T.astype(BF16)

    pl.semaphore_wait(barrier, len(peers))

    act_k = count[0]
    count[0] += 2

    def swap(half):
        k = act_k + half

        def start(i, _):
            pltpu.make_async_remote_copy(
                src_ref=cols(i, half, 1 - c), dst_ref=abuf.at[16 * half + i, 1], send_sem=ss.at[k], recv_sem=rs.at[k],
                device_id=sib, device_id_type=MESH,
            ).start()
            return 0

        lax.fori_loop(0, 16, start, 0)
        part = abuf.at[16 * half:16 * half + 16]
        whole = pltpu.make_async_remote_copy(
            src_ref=part.at[:, 0], dst_ref=part.at[:, 1], send_sem=ss.at[k], recv_sem=rs.at[k],
            device_id=sib, device_id_type=MESH,
        )
        sent.append(whole)
        return whole

    s_copy = send(sgt.at[0], sgt.at[1], sib)
    swap_a = swap(1)
    g_r = send(act.at[:, 0:FBLK], gblk.at[1], right)
    g_l = send(act.at[:, 0:FBLK], gblk.at[2], left)
    swap_b = swap(0)
    w_y = [send(kw.at[part], wbuf.at[y, zh, c, part], to) for to in ys]
    l_copies = [send(lt.at[0], lt.at[1 + i], to) for i, to in enumerate(group)]

    own_all.wait()
    s_copy.wait_recv()
    heads = jnp.concatenate([sgt[0], sgt[1]], axis=1)

    def block(i):
        return jnp.dot(heads, abuf[i].reshape(2 * T, T), preferred_element_type=F32)

    def block_b(i, _):
        yb[lax.div(i, 2), pl.ds(pl.multiple_of(lax.rem(i, 2) * T, T), T)] = block(i)
        return 0

    def block_a(i, _):
        psum[:, i] = block(16 + i).reshape(X, 32, T)
        return 0

    def y_step(buf, up_buf, down_buf, s, before):
        n = buf.shape[1] // 2
        t = 4 - s
        hi, lo = lax.rem(y + t, Y), lax.rem(y + Y - t, Y)
        if s == 0:
            return [
                send(buf.at[hi, 0:n], up_buf.at[0, 0:n], up),
                send(buf.at[hi, n:2 * n], down_buf.at[0, n:2 * n], down),
            ]
        before[0].wait_recv()
        if s == 1:
            buf[hi, 0:n] += up_buf[0, 0:n]
        else:
            buf[hi] += up_buf[s - 1]
        a = send(buf.at[hi], up_buf.at[s], up)
        before[1].wait_recv()
        if s == 1:
            buf[lo, n:2 * n] += down_buf[0, n:2 * n]
        else:
            buf[lo] += down_buf[s - 1]
        b = send(buf.at[lo], down_buf.at[s], down)
        return [a, b]

    def step_b(s, before):
        return y_step(yb, ybr, ybl, s, before)

    def step_a(s, before):
        return y_step(ya, yar, yal, s, before)

    def step_f(s, before):
        return y_step(yf, yfr, yfl, s, before)

    xp, xm, xo = lax.rem(x + 1, X), lax.rem(x + 3, X), lax.rem(x + 2, X)
    swap_a.wait_recv()
    lax.fori_loop(0, 16, block_a, 0)
    r1 = send(psum.at[xo, 0:8], xr.at[0], right)
    l1 = send(psum.at[xo, 8:16], xr.at[1], left)
    blk_copy.wait()
    g_s = [send(gblk.at[0], gblk.at[3], sib)]
    swap_b.wait_recv()
    lax.fori_loop(0, 16, block_b, 0)
    b_y = step_b(0, None)

    g_r.wait_recv()
    f_r = send(gblk.at[1, 0:64], gblk.at[6, 0:64], right)
    g_l.wait_recv()
    f_l = send(gblk.at[2, 64:128], gblk.at[6, 64:128], left)
    g_s.append(send(gblk.at[1], gblk.at[4], sib))
    g_s.append(send(gblk.at[2], gblk.at[5], sib))
    r2 = send(psum.at[xp, 8:16], xr.at[2], right)
    l2 = send(psum.at[xm, 0:8], xr.at[3], left)

    w_copy.wait()
    arrived(w_y)
    w_z = [
        send(wbuf.at[:, zh, c, part], wbuf.at[:, zh, c, part], fore),
        send(wbuf.at[:, zh, c, part], wbuf.at[:, zh, c, part], back),
    ]

    arrived(l_copies)
    every = lt[...]
    cy[0, 0:8] = jnp.sum(every, axis=0).astype(F32)
    cy[0, 8:16] = jnp.sum((every > 0).astype(jnp.int32), axis=0).astype(F32)
    y_counts = [send(cy.at[0], cy.at[1 + i], to) for i, to in enumerate(ys)]

    mine = pl.ds(pl.multiple_of((2 * x + c) * T, T), T)

    def weigh(s):
        weighted = gblk[s, :, mine].astype(F32) * ratio_of(lt[s])
        wbt[:, s * T:(s + 1) * T] = weighted.T.astype(BF16)

    for s in range(3):
        weigh(s)
    r1.wait_recv()
    psum[xp, 0:8] += xr[0]
    r3 = send(psum.at[xp, 0:8], xr.at[4], right)
    l1.wait_recv()
    psum[xm, 8:16] += xr[1]
    l3 = send(psum.at[xm, 8:16], xr.at[5], left)
    b_y = step_b(1, b_y)
    for s in range(3):
        g_s[s].wait_recv()
        weigh(3 + s)

    def rows_of(lo, hi, i):
        return gblk[lo:hi, :, pl.ds(pl.multiple_of(i * T, T), T)].reshape((hi - lo) * T, T)

    def factor_first(i, _):
        yf[i] = jnp.dot(wbt[:, 0:6 * T], rows_of(0, 6, i), preferred_element_type=F32)
        return 0

    def factor_rest(i, _):
        yf[i] += jnp.dot(wbt[:, 6 * T:8 * T], rows_of(6, 8, i), preferred_element_type=F32)
        return 0

    lax.fori_loop(0, Y, factor_first, 0)
    arrived(y_counts)
    cz[0] = jnp.sum(cy[...], axis=0)
    z_counts = [send(cz.at[0], cz.at[1 + i], to) for i, to in enumerate(zhs)]
    arrived([f_r, f_l])
    g_s.append(send(gblk.at[6], gblk.at[7], sib))
    weigh(6)
    g_s[3].wait_recv()
    weigh(7)
    lax.fori_loop(0, Y, factor_rest, 0)
    f_y = step_f(0, None)
    b_y = step_b(2, b_y)

    l2.wait_recv()
    r3.wait_recv()
    ya[0:4] = (psum[x, 0:8] + xr[3] + xr[4]).reshape(4, 64, T)
    r2.wait_recv()
    l3.wait_recv()
    ya[4:8] = (psum[x, 8:16] + xr[2] + xr[5]).reshape(4, 64, T)
    a_y = step_a(0, None)
    arrived(w_z)
    zp, zm = lax.rem(zh + 1, ZH), lax.rem(zh + 3, ZH)
    w_z = [
        send(wbuf.at[0:4, zm, c, part], wbuf.at[0:4, zm, c, part], fore),
        send(wbuf.at[4:8, zp, c, part], wbuf.at[4:8, zp, c, part], back),
    ]
    f_y = step_f(1, f_y)
    b_y = step_b(3, b_y)
    a_y = step_a(1, a_y)
    arrived(z_counts)
    cl[0] = jnp.sum(cz[...], axis=0)
    l_counts = [send(cl.at[0], cl.at[1 + i], to) for i, to in enumerate(zls)]
    f_y = step_f(2, f_y)

    def quarter(q, lo=0, hi=Y):
        rows = pl.ds(pl.multiple_of(32 * q, 32), 32)
        return wbuf.at[lo:hi, :, c, rows]

    arrived(w_z)
    w_x = [send(quarter(x), quarter(x), right), send(quarter(x), quarter(x), left)]
    w_s = [send(quarter(x), quarter(x), sib)]

    arrived(b_y)
    xb[...] = jnp.swapaxes((yb[y] + ybr[3] + ybl[3]).reshape(2, X, 32, T), 0, 1)
    b_x = [send(xb.at[lax.rem(x + 1 + i, X)], xbr.at[1 + i], (to)) for i, to in enumerate([right, dev(dx=2), left])]
    xbr[0] = xb[x]
    a_y = step_a(2, a_y)
    f_y = step_f(3, f_y)
    a_y = step_a(3, a_y)

    arrived(l_counts)
    total = cl[0] + cl[1] + cl[2]
    valid = jnp.sum(total[0:8], axis=0, keepdims=True)
    seqs = jnp.sum(total[8:16], axis=0, keepdims=True)
    scale_row = valid / seqs
    scale = jnp.max(scale_row)

    arrived(w_x)
    w_x = [send(quarter(xm, 0, 4), quarter(xm, 0, 4), right), send(quarter(xp, 4, 8), quarter(xp, 4, 8), left)]
    w_s += [send(quarter(xm), quarter(xm), sib), send(quarter(xp), quarter(xp), sib)]

    arrived(f_y)
    zf[...] = (yf[y] + yfr[3] + yfl[3]).T.reshape(ZH, 32, T)
    f_z = [send(zf.at[lax.rem(zh + 1 + i, ZH)], zfr.at[1 + i], to) for i, to in enumerate(zhs)]
    zfr[0] = zf[zh]
    arrived(b_x)
    zw[0:2] = xbr[0] + xbr[1] + xbr[2] + xbr[3]
    arrived(a_y)
    zw[2:4] = (ya[y] + yar[3] + yal[3]).reshape(2, 32, T)
    w_zs = [send(zw.at[lax.rem(zh + 1 + i, ZH)], zwr.at[1 + i], to) for i, to in enumerate(zhs)]
    zwr[0] = zw[zh]

    arrived(w_x)
    w_s.append(send(quarter(xo), quarter(xo), sib))

    def product(i):
        out = lax.dot_general(
            sgs[...], wbuf[i].reshape(1024, T), (((1,), (1,)), ((), ())), preferred_element_type=F32
        )
        grad_in[:, i * 1024:(i + 1) * 1024] = (scale * out).astype(BF16)

    arrived(f_z)
    lr[0, 32:64] = zfr[0] + zfr[1] + zfr[2] + zfr[3]
    arrived(w_zs)
    lr[0, 0:32] = zwr[0] + zwr[1] + zwr[2] + zwr[3]
    l_sums = [send(lr.at[0], lr.at[1 + i], to) for i, to in enumerate(zls)]
    arrived(w_s)
    for i in range(3):
        product(i)
    arrived(l_sums)
    done = lr[0] + lr[1] + lr[2]
    finw[...] = done[0:32]
    finf[...] = done[32:64].reshape(2, 16, T)
    slot = 2 * x + c
    last = [send(finw, fw.at[x], to) for to in same]
    last += [send(finf.at[c], ff.at[slot], to) for to in same]
    last += [send(finf.at[1 - c], ff.at[slot], to) for to in other]
    fw[x] = done[0:32]
    ff[slot] = finf[c]
    for i in range(3, 8):
        product(i)
    arrived(last)
    wgrad[...] = scale * fw[...].reshape(T, T).T
    for g in range(8):
        factor[:, g * T:(g + 1) * T] = ff[g] / seqs
    for copy in sent:
        copy.wait_send()


def shards(activations, out_grad, key_weight, lengths):
    sems = 136
    hbm = pl.BlockSpec(memory_space=pltpu.HBM)
    vmem = pl.BlockSpec(memory_space=pltpu.VMEM)
    return pl.pallas_call(
        kernel,
        out_shape=(
            jax.ShapeDtypeStruct((T, 8192), BF16),
            jax.ShapeDtypeStruct((T, T), F32),
            jax.ShapeDtypeStruct((16, FBLK), F32),
        ),
        in_specs=[hbm, hbm, hbm, hbm],
        out_specs=(vmem, vmem, vmem),
        scratch_shapes=[
            pltpu.VMEM((32, 2, T, T), BF16),
            pltpu.VMEM((2, T, T), BF16),
            pltpu.VMEM((T, T), BF16),
            pltpu.VMEM((X, 16, 32, T), F32),
            pltpu.VMEM((6, 8, 32, T), F32),
            pltpu.VMEM((Y, 256, T), F32),
            pltpu.VMEM((4, 256, T), F32),
            pltpu.VMEM((4, 256, T), F32),
            pltpu.VMEM((Y, 64, T), F32),
            pltpu.VMEM((4, 64, T), F32),
            pltpu.VMEM((4, 64, T), F32),
            pltpu.VMEM((Y, T, T), F32),
            pltpu.VMEM((4, T, T), F32),
            pltpu.VMEM((4, T, T), F32),
            pltpu.VMEM((X, 2, 32, T), F32),
            pltpu.VMEM((X, 2, 32, T), F32),
            pltpu.VMEM((8, T, FBLK), BF16),
            pltpu.VMEM((T, 8 * T), BF16),
            pltpu.VMEM((8, 8, T), jnp.int32),
            pltpu.VMEM((Y, 16, T), F32),
            pltpu.VMEM((ZH, 16, T), F32),
            pltpu.VMEM((ZL, 16, T), F32),
            pltpu.VMEM((Y, ZH, 2, T, T), BF16),
            pltpu.VMEM((ZH, 32, T), F32),
            pltpu.VMEM((ZH, 32, T), F32),
            pltpu.VMEM((ZH, 32, T), F32),
            pltpu.VMEM((ZH, 32, T), F32),
            pltpu.VMEM((ZL, 64, T), F32),
            pltpu.VMEM((32, T), F32),
            pltpu.VMEM((2, 16, T), F32),
            pltpu.VMEM((X, 32, T), F32),
            pltpu.VMEM((8, 16, T), F32),
            pltpu.VMEM((T, T), BF16),
            pltpu.SMEM((1, 8), jnp.int32),
            pltpu.SemaphoreType.DMA((sems,)),
            pltpu.SemaphoreType.DMA((sems,)),
            pltpu.SemaphoreType.DMA((8,)),
        ],
        compiler_params=pltpu.CompilerParams(
            collective_id=0, has_side_effects=True, vmem_limit_bytes=48 * 1024 * 1024
        ),
    )(*[pltpu.with_memory_space_constraint(a, pltpu.HBM) for a in (activations, out_grad, key_weight, lengths)])


def solution(mesh):
    in_specs = (
        P(("rep", "fsdp"), None),
        P(("rep", "fsdp"), None),
        P("fsdp", None),
        P(("rep", "fsdp"), None),
    )
    out_specs = (P(("rep", "fsdp"), None), P("fsdp", None), P("fsdp", None))
    return jax.shard_map(shards, mesh=mesh, in_specs=in_specs, out_specs=out_specs, check_vma=False)
```

```python
import jax
import jax.numpy as jnp
from jax import lax
from jax.experimental import pallas as pl
from jax.experimental.pallas import tpu as pltpu
from jax.sharding import PartitionSpec as P

FBLK = 1024
X, Y, ZH, ZL = 4, 8, 4, 3
T = 128
MESH = pl.DeviceIdType.MESH
F32, BF16 = jnp.float32, jnp.bfloat16


def ratio_of(tile):
    pos = lax.broadcasted_iota(jnp.int32, (T, T), 0)
    end = jnp.zeros((1, T), jnp.int32)
    ratio = jnp.zeros((T, T), F32)
    for s in range(8):
        length = tile[s:s + 1, :]
        start, end = end, end + length
        inverse = 1.0 / jnp.maximum(length, 1).astype(F32)
        ratio = ratio + jnp.where((pos >= start) & (pos < end), inverse, 0.0)
    return ratio


def kernel(
    act, og, kw, lens, grad_in, wgrad, factor,
    abuf, sgt, sgs, psum, xr, yb, ybr, ybl, ya, yar, yal, yf, yfr, yfl, xb, xbr, gblk, wbt, lt, cy, cz, cl,
    wbuf, zw, zwr, zf, zfr, lr, finw, finf, fw, ff, ogv, lens_s, ss, rs, ls,
):
    rep, fs = lax.axis_index("rep"), lax.axis_index("fsdp")
    x, zl = lax.div(rep, ZL), lax.rem(rep, ZL)
    y, zh, c = lax.div(fs, 8), lax.rem(lax.div(fs, 2), ZH), lax.rem(fs, 2)

    def dev(dx=0, dy=0, dzh=0, dzl=0, dc=0):
        c2 = 1 - c if dc else c
        x2, y2, zh2, zl2 = lax.rem(x + dx, X), lax.rem(y + dy, Y), lax.rem(zh + dzh, ZH), lax.rem(zl + dzl, ZL)
        return (x2 * ZL + zl2, y2 * 8 + zh2 * 2 + c2)

    sib, right, left = dev(dc=1), dev(dx=1), dev(dx=3)
    up, down = dev(dy=1), dev(dy=7)
    fore, back = dev(dzh=1), dev(dzh=3)
    group = [right, left, sib, dev(dx=1, dc=1), dev(dx=3, dc=1), dev(dx=2), dev(dx=2, dc=1)]
    same, other = [group[0], group[1], group[5]], [group[2], group[3], group[4], group[6]]
    ys = [dev(dy=d) for d in range(1, Y)]
    zhs = [dev(dzh=d) for d in range(1, ZH)]
    zls = [dev(dzl=d) for d in range(1, ZL)]
    count = [0]
    sent = []

    def send(src, dst, to):
        k = count[0]
        count[0] += 1
        copy = pltpu.make_async_remote_copy(
            src_ref=src, dst_ref=dst, send_sem=ss.at[k], recv_sem=rs.at[k],
            device_id=to, device_id_type=MESH,
        )
        copy.start()
        sent.append(copy)
        return copy

    def arrived(copies):
        for copy in copies:
            copy.wait_recv()

    lens_copy = pltpu.make_async_copy(lens, lens_s, ls.at[4])
    lens_copy.start()
    og_copy = pltpu.make_async_copy(og, ogv, ls.at[1])
    og_copy.start()

    barrier = pltpu.get_barrier_semaphore()
    peers = group + ys + zhs + zls
    for peer in peers:
        pl.semaphore_signal(barrier, inc=1, device_id=peer, device_id_type=MESH)

    def cols(i, half, core):
        if half == 0:
            b = lax.rem(i, 8) * 8 + lax.div(i, 8) * 2 + core
        else:
            b = lax.div(i, 2) * 8 + 4 + lax.rem(i, 2) * 2 + core
        return act.at[:, pl.ds(pl.multiple_of(b * T, T), T)]

    for half in range(2):
        def start_own(i, _, half=half):
            pltpu.make_async_copy(cols(i, half, c), abuf.at[16 * half + i, 0], ls.at[0]).start()
            return 0

        lax.fori_loop(0, 16, start_own, 0)
    own_all = pltpu.make_async_copy(abuf.at[:, 0], abuf.at[:, 0], ls.at[0])
    blk_copy = pltpu.make_async_copy(act.at[:, 0:FBLK], gblk.at[0], ls.at[3])
    blk_copy.start()
    part = pl.ds(pl.multiple_of(32 * x, 32), 32)
    w_copy = pltpu.make_async_copy(kw.at[part], wbuf.at[y, zh, c, part], ls.at[2])
    w_copy.start()

    pl.semaphore_wait(barrier, len(peers))

    act_k = count[0]
    count[0] += 2

    def swap(half):
        k = act_k + half

        def start(i, _):
            pltpu.make_async_remote_copy(
                src_ref=cols(i, half, 1 - c), dst_ref=abuf.at[16 * half + i, 1], send_sem=ss.at[k], recv_sem=rs.at[k],
                device_id=sib, device_id_type=MESH,
            ).start()
            return 0

        lax.fori_loop(0, 16, start, 0)
        part = abuf.at[16 * half:16 * half + 16]
        whole = pltpu.make_async_remote_copy(
            src_ref=part.at[:, 0], dst_ref=part.at[:, 1], send_sem=ss.at[k], recv_sem=rs.at[k],
            device_id=sib, device_id_type=MESH,
        )
        sent.append(whole)
        return whole

    g_r = send(act.at[:, 0:FBLK], gblk.at[1], right)
    g_l = send(act.at[:, 0:FBLK], gblk.at[2], left)
    swap_b = swap(0)
    swap_a = swap(1)
    w_y = [send(kw.at[part], wbuf.at[y, zh, c, part], to) for to in ys]
    lens_copy.wait()
    row = lax.broadcasted_iota(jnp.int32, (8, T), 0)
    tile = jnp.zeros((8, T), jnp.int32)
    for s in range(8):
        tile = jnp.where(row == s, lens_s[0, s], tile)
    lt[0] = tile
    og_copy.wait()
    scaled = ogv[...].astype(F32) * ratio_of(tile)
    sgs[...] = scaled.astype(BF16)
    sgt[0] = scaled.T.astype(BF16)
    s_copy = send(sgt.at[0], sgt.at[1], sib)
    l_copies = [send(lt.at[0], lt.at[1 + i], to) for i, to in enumerate(group)]

    own_all.wait()
    s_copy.wait_recv()
    heads = jnp.concatenate([sgt[0], sgt[1]], axis=1)

    def block(i):
        return jnp.dot(heads, abuf[i].reshape(2 * T, T), preferred_element_type=F32)

    def block_b(i, _):
        yb[lax.div(i, 8), lax.rem(i, 8)] = block(i)
        return 0

    def block_a(i, _):
        psum[:, i] = block(16 + i).reshape(X, 32, T)
        return 0

    def y_step(buf, up_buf, down_buf, s, before):
        n = buf.shape[-2] // 2
        t = 4 - s
        hi, lo = lax.rem(y + t, Y), lax.rem(y + Y - t, Y)
        if s == 0:
            return [
                send(buf.at[hi, 0:n], up_buf.at[0, 0:n], up),
                send(buf.at[hi, n:2 * n], down_buf.at[0, n:2 * n], down),
            ]
        before[0].wait_recv()
        if s == 1:
            buf[hi, 0:n] += up_buf[0, 0:n]
        else:
            buf[hi] += up_buf[s - 1]
        a = send(buf.at[hi], up_buf.at[s], up)
        before[1].wait_recv()
        if s == 1:
            buf[lo, n:2 * n] += down_buf[0, n:2 * n]
        else:
            buf[lo] += down_buf[s - 1]
        b = send(buf.at[lo], down_buf.at[s], down)
        return [a, b]

    def step_b(k, s, before):
        return y_step(yb.at[k], ybr.at[k], ybl.at[k], s, before)

    def step_a(s, before):
        return y_step(ya, yar, yal, s, before)

    def step_f(s, before):
        return y_step(yf, yfr, yfl, s, before)

    xp, xm, xo = lax.rem(x + 1, X), lax.rem(x + 3, X), lax.rem(x + 2, X)
    swap_b.wait_recv()
    lax.fori_loop(0, 8, block_b, 0, unroll=4)
    b0 = step_b(0, 0, None)
    lax.fori_loop(8, 16, block_b, 0, unroll=4)
    b1 = step_b(1, 0, None)
    swap_a.wait_recv()
    lax.fori_loop(0, 16, block_a, 0, unroll=4)
    r1 = send(psum.at[xo, 0:8], xr.at[0], right)
    l1 = send(psum.at[xo, 8:16], xr.at[1], left)
    blk_copy.wait()
    g_s = [send(gblk.at[0], gblk.at[3], sib)]
    w_copy.wait()
    arrived(w_y)
    w_z = [
        send(wbuf.at[:, zh, c, part], wbuf.at[:, zh, c, part], fore),
        send(wbuf.at[:, zh, c, part], wbuf.at[:, zh, c, part], back),
    ]
    g_r.wait_recv()
    f_r = send(gblk.at[1, 0:64], gblk.at[6, 0:64], right)
    g_l.wait_recv()
    f_l = send(gblk.at[2, 64:128], gblk.at[6, 64:128], left)
    g_s.append(send(gblk.at[1], gblk.at[4], sib))
    g_s.append(send(gblk.at[2], gblk.at[5], sib))

    b0 = step_b(0, 1, b0)
    b1 = step_b(1, 1, b1)
    r2 = send(psum.at[xp, 8:16], xr.at[2], right)
    l2 = send(psum.at[xm, 0:8], xr.at[3], left)

    arrived(l_copies)
    every = lt[...]
    cy[0, 0:8] = jnp.sum(every, axis=0).astype(F32)
    cy[0, 8:16] = jnp.sum((every > 0).astype(jnp.int32), axis=0).astype(F32)
    y_counts = [send(cy.at[0], cy.at[1 + i], to) for i, to in enumerate(ys)]

    mine = pl.ds(pl.multiple_of((2 * x + c) * T, T), T)

    def weigh(s):
        weighted = gblk[s, :, mine].astype(F32) * ratio_of(lt[s])
        wbt[:, s * T:(s + 1) * T] = weighted.T.astype(BF16)

    def rows_of(lo, hi, i):
        return gblk[lo:hi, :, pl.ds(pl.multiple_of(i * T, T), T)].reshape((hi - lo) * T, T)

    def factor_first(i, _):
        yf[i] = jnp.dot(wbt[:, 0:6 * T], rows_of(0, 6, i), preferred_element_type=F32)
        return 0

    def factor_rest(i, _):
        yf[i] += jnp.dot(wbt[:, 6 * T:8 * T], rows_of(6, 8, i), preferred_element_type=F32)
        return 0

    for s in range(3):
        weigh(s)
    for s in range(3):
        g_s[s].wait_recv()
        weigh(3 + s)
    lax.fori_loop(0, Y, factor_first, 0, unroll=4)
    arrived([f_r, f_l])
    g_s.append(send(gblk.at[6], gblk.at[7], sib))
    r1.wait_recv()
    psum[xp, 0:8] += xr[0]
    r3 = send(psum.at[xp, 0:8], xr.at[4], right)
    l1.wait_recv()
    psum[xm, 8:16] += xr[1]
    l3 = send(psum.at[xm, 8:16], xr.at[5], left)
    b0 = step_b(0, 2, b0)
    b1 = step_b(1, 2, b1)
    weigh(6)
    g_s[3].wait_recv()
    weigh(7)
    lax.fori_loop(0, Y, factor_rest, 0, unroll=4)
    f_y = step_f(0, None)
    b0 = step_b(0, 3, b0)
    b1 = step_b(1, 3, b1)
    arrived(y_counts)
    cz[0] = jnp.sum(cy[...], axis=0)
    z_counts = [send(cz.at[0], cz.at[1 + i], to) for i, to in enumerate(zhs)]
    arrived(w_z)
    zp, zm = lax.rem(zh + 1, ZH), lax.rem(zh + 3, ZH)
    w_z = [
        send(wbuf.at[0:4, zm, c, part], wbuf.at[0:4, zm, c, part], fore),
        send(wbuf.at[4:8, zp, c, part], wbuf.at[4:8, zp, c, part], back),
    ]
    l2.wait_recv()
    r3.wait_recv()
    ya[0:4] = (psum[x, 0:8] + xr[3] + xr[4]).reshape(4, 64, T)
    r2.wait_recv()
    l3.wait_recv()
    ya[4:8] = (psum[x, 8:16] + xr[2] + xr[5]).reshape(4, 64, T)
    a_y = step_a(0, None)
    f_y = step_f(1, f_y)
    a_y = step_a(1, a_y)
    b_x = []
    for k, arriving in enumerate([b0, b1]):
        arrived(arriving)
        xb[k] = (yb[k, y] + ybr[k, 3] + ybl[k, 3]).reshape(X, 32, T)
        b_x += [send(xb.at[k, lax.rem(x + 1 + i, X)], xbr.at[k, 1 + i], to) for i, to in enumerate([right, dev(dx=2), left])]
        xbr[k, 0] = xb[k, x]
    arrived(z_counts)
    cl[0] = jnp.sum(cz[...], axis=0)
    l_counts = [send(cl.at[0], cl.at[1 + i], to) for i, to in enumerate(zls)]
    f_y = step_f(2, f_y)

    def quarter(q, lo=0, hi=Y):
        rows = pl.ds(pl.multiple_of(32 * q, 32), 32)
        return wbuf.at[lo:hi, :, c, rows]

    arrived(w_z)
    w_x = [send(quarter(x), quarter(x), right), send(quarter(x), quarter(x), left)]
    w_s = [send(quarter(x), quarter(x), sib)]
    a_y = step_a(2, a_y)
    f_y = step_f(3, f_y)
    a_y = step_a(3, a_y)

    arrived(l_counts)
    total = cl[0] + cl[1] + cl[2]
    valid = jnp.sum(total[0:8], axis=0, keepdims=True)
    seqs = jnp.sum(total[8:16], axis=0, keepdims=True)
    scale_row = valid / seqs
    scale = jnp.max(scale_row)

    arrived(f_y)
    zf[...] = (yf[y] + yfr[3] + yfl[3]).T.reshape(ZH, 32, T)
    f_z = [send(zf.at[lax.rem(zh + 1 + i, ZH)], zfr.at[1 + i], to) for i, to in enumerate(zhs)]
    zfr[0] = zf[zh]
    arrived(b_x)
    zw[0:2] = xbr[:, 0] + xbr[:, 1] + xbr[:, 2] + xbr[:, 3]
    arrived(a_y)
    zw[2:4] = (ya[y] + yar[3] + yal[3]).reshape(2, 32, T)
    w_zs = [send(zw.at[lax.rem(zh + 1 + i, ZH)], zwr.at[1 + i], to) for i, to in enumerate(zhs)]
    zwr[0] = zw[zh]
    arrived(w_x)
    w_x = [send(quarter(xm, 0, 4), quarter(xm, 0, 4), right), send(quarter(xp, 4, 8), quarter(xp, 4, 8), left)]
    w_s += [send(quarter(xm), quarter(xm), sib), send(quarter(xp), quarter(xp), sib)]

    arrived(w_x)
    w_s.append(send(quarter(xo), quarter(xo), sib))

    def product(i):
        out = lax.dot_general(
            sgs[...], wbuf[i].reshape(1024, T), (((1,), (1,)), ((), ())), preferred_element_type=F32
        )
        grad_in[:, i * 1024:(i + 1) * 1024] = (scale * out).astype(BF16)

    arrived(f_z)
    lr[0, 32:64] = zfr[0] + zfr[1] + zfr[2] + zfr[3]
    arrived(w_zs)
    lr[0, 0:32] = zwr[0] + zwr[1] + zwr[2] + zwr[3]
    l_sums = [send(lr.at[0], lr.at[1 + i], to) for i, to in enumerate(zls)]
    arrived(w_s)
    for i in range(3):
        product(i)
    arrived(l_sums)
    done = lr[0] + lr[1] + lr[2]
    finw[...] = done[0:32]
    finf[...] = done[32:64].reshape(2, 16, T)
    slot = 2 * x + c
    last = [send(finw, fw.at[x], to) for to in same]
    last += [send(finf.at[c], ff.at[slot], to) for to in same]
    last += [send(finf.at[1 - c], ff.at[slot], to) for to in other]
    fw[x] = done[0:32]
    ff[slot] = finf[c]
    for i in range(3, 8):
        product(i)
    arrived(last)
    wgrad[...] = scale * fw[...].reshape(T, T).T
    for g in range(8):
        factor[:, g * T:(g + 1) * T] = ff[g] / seqs
    for copy in sent:
        copy.wait_send()


def shards(activations, out_grad, key_weight, lengths):
    sems = 152
    hbm = pl.BlockSpec(memory_space=pltpu.HBM)
    vmem = pl.BlockSpec(memory_space=pltpu.VMEM)
    return pl.pallas_call(
        kernel,
        out_shape=(
            jax.ShapeDtypeStruct((T, 8192), BF16),
            jax.ShapeDtypeStruct((T, T), F32),
            jax.ShapeDtypeStruct((16, FBLK), F32),
        ),
        in_specs=[hbm, hbm, hbm, hbm],
        out_specs=(vmem, vmem, vmem),
        scratch_shapes=[
            pltpu.VMEM((32, 2, T, T), BF16),
            pltpu.VMEM((2, T, T), BF16),
            pltpu.VMEM((T, T), BF16),
            pltpu.VMEM((X, 16, 32, T), F32),
            pltpu.VMEM((6, 8, 32, T), F32),
            pltpu.VMEM((2, Y, T, T), F32),
            pltpu.VMEM((2, 4, T, T), F32),
            pltpu.VMEM((2, 4, T, T), F32),
            pltpu.VMEM((Y, 64, T), F32),
            pltpu.VMEM((4, 64, T), F32),
            pltpu.VMEM((4, 64, T), F32),
            pltpu.VMEM((Y, T, T), F32),
            pltpu.VMEM((4, T, T), F32),
            pltpu.VMEM((4, T, T), F32),
            pltpu.VMEM((2, X, 32, T), F32),
            pltpu.VMEM((2, X, 32, T), F32),
            pltpu.VMEM((8, T, FBLK), BF16),
            pltpu.VMEM((T, 8 * T), BF16),
            pltpu.VMEM((8, 8, T), jnp.int32),
            pltpu.VMEM((Y, 16, T), F32),
            pltpu.VMEM((ZH, 16, T), F32),
            pltpu.VMEM((ZL, 16, T), F32),
            pltpu.VMEM((Y, ZH, 2, T, T), BF16),
            pltpu.VMEM((ZH, 32, T), F32),
            pltpu.VMEM((ZH, 32, T), F32),
            pltpu.VMEM((ZH, 32, T), F32),
            pltpu.VMEM((ZH, 32, T), F32),
            pltpu.VMEM((ZL, 64, T), F32),
            pltpu.VMEM((32, T), F32),
            pltpu.VMEM((2, 16, T), F32),
            pltpu.VMEM((X, 32, T), F32),
            pltpu.VMEM((8, 16, T), F32),
            pltpu.VMEM((T, T), BF16),
            pltpu.SMEM((1, 8), jnp.int32),
            pltpu.SemaphoreType.DMA((sems,)),
            pltpu.SemaphoreType.DMA((sems,)),
            pltpu.SemaphoreType.DMA((8,)),
        ],
        compiler_params=pltpu.CompilerParams(
            collective_id=0, has_side_effects=True, vmem_limit_bytes=48 * 1024 * 1024
        ),
    )(*[pltpu.with_memory_space_constraint(a, pltpu.HBM) for a in (activations, out_grad, key_weight, lengths)])


def solution(mesh):
    in_specs = (
        P(("rep", "fsdp"), None),
        P(("rep", "fsdp"), None),
        P("fsdp", None),
        P(("rep", "fsdp"), None),
    )
    out_specs = (P(("rep", "fsdp"), None), P("fsdp", None), P("fsdp", None))
    return jax.shard_map(shards, mesh=mesh, in_specs=in_specs, out_specs=out_specs, check_vma=False)
```

```python
import jax
import jax.numpy as jnp
from jax import lax
from jax.experimental import pallas as pl
from jax.experimental.pallas import tpu as pltpu
from jax.sharding import PartitionSpec as P

FBLK = 1024
X, Y, ZH, ZL = 4, 8, 4, 3
T = 128
MESH = pl.DeviceIdType.MESH
F32, BF16 = jnp.float32, jnp.bfloat16


def ratio_of(tile):
    pos = lax.broadcasted_iota(jnp.int32, (T, T), 0)
    end = jnp.zeros((1, T), jnp.int32)
    ratio = jnp.zeros((T, T), F32)
    for s in range(8):
        length = tile[s:s + 1, :]
        start, end = end, end + length
        inverse = 1.0 / jnp.maximum(length, 1).astype(F32)
        ratio = ratio + jnp.where((pos >= start) & (pos < end), inverse, 0.0)
    return ratio


def kernel(
    act, og, kw, lens, grad_in, wgrad, factor,
    abuf, sgt, sgs, psum, xr, yb, ybr, ybl, ya, yar, yal, yf, yfr, yfl, xb, xbr, gblk, wbt, lt, cy, cz, cl,
    wbuf, zw, zwr, zf, zfr, lr, finw, finf, fw, ff, ogv, lens_s, ss, rs, ls,
):
    rep, fs = lax.axis_index("rep"), lax.axis_index("fsdp")
    x, zl = lax.div(rep, ZL), lax.rem(rep, ZL)
    y, zh, c = lax.div(fs, 8), lax.rem(lax.div(fs, 2), ZH), lax.rem(fs, 2)

    def dev(dx=0, dy=0, dzh=0, dzl=0, dc=0):
        c2 = 1 - c if dc else c
        x2, y2, zh2, zl2 = lax.rem(x + dx, X), lax.rem(y + dy, Y), lax.rem(zh + dzh, ZH), lax.rem(zl + dzl, ZL)
        return (x2 * ZL + zl2, y2 * 8 + zh2 * 2 + c2)

    sib, right, left = dev(dc=1), dev(dx=1), dev(dx=3)
    up, down = dev(dy=1), dev(dy=7)
    fore, back = dev(dzh=1), dev(dzh=3)
    group = [right, left, sib, dev(dx=1, dc=1), dev(dx=3, dc=1), dev(dx=2), dev(dx=2, dc=1)]
    same, other = [group[0], group[1], group[5]], [group[2], group[3], group[4], group[6]]
    ys = [dev(dy=d) for d in range(1, Y)]
    zhs = [dev(dzh=d) for d in range(1, ZH)]
    zls = [dev(dzl=d) for d in range(1, ZL)]
    count = [0]
    sent = []

    def send(src, dst, to):
        k = count[0]
        count[0] += 1
        copy = pltpu.make_async_remote_copy(
            src_ref=src, dst_ref=dst, send_sem=ss.at[k], recv_sem=rs.at[k],
            device_id=to, device_id_type=MESH,
        )
        copy.start()
        sent.append(copy)
        return copy

    def arrived(copies):
        for copy in copies:
            copy.wait_recv()

    lens_copy = pltpu.make_async_copy(lens, lens_s, ls.at[4])
    lens_copy.start()
    og_copy = pltpu.make_async_copy(og, ogv, ls.at[1])
    og_copy.start()

    barrier = pltpu.get_barrier_semaphore()
    peers = group + ys + zhs + zls
    for peer in peers:
        pl.semaphore_signal(barrier, inc=1, device_id=peer, device_id_type=MESH)

    def cols(i, half, core):
        if half == 0:
            b = lax.rem(i, 8) * 8 + lax.div(i, 8) * 2 + core
        else:
            b = lax.div(i, 2) * 8 + 4 + lax.rem(i, 2) * 2 + core
        return act.at[:, pl.ds(pl.multiple_of(b * T, T), T)]

    for half in range(2):
        def start_own(i, _, half=half):
            pltpu.make_async_copy(cols(i, half, c), abuf.at[16 * half + i, 0], ls.at[0]).start()
            return 0

        lax.fori_loop(0, 16, start_own, 0)
    own_all = pltpu.make_async_copy(abuf.at[:, 0], abuf.at[:, 0], ls.at[0])
    blk_copy = pltpu.make_async_copy(act.at[:, 0:FBLK], gblk.at[0], ls.at[3])
    blk_copy.start()
    part = pl.ds(pl.multiple_of(32 * x, 32), 32)
    w_copy = pltpu.make_async_copy(kw.at[part], wbuf.at[y, zh, c, part], ls.at[2])
    w_copy.start()

    pl.semaphore_wait(barrier, len(peers))

    act_k = count[0]
    count[0] += 2

    def swap(half):
        k = act_k + half

        def start(i, _):
            pltpu.make_async_remote_copy(
                src_ref=cols(i, half, 1 - c), dst_ref=abuf.at[16 * half + i, 1], send_sem=ss.at[k], recv_sem=rs.at[k],
                device_id=sib, device_id_type=MESH,
            ).start()
            return 0

        lax.fori_loop(0, 16, start, 0)
        part = abuf.at[16 * half:16 * half + 16]
        whole = pltpu.make_async_remote_copy(
            src_ref=part.at[:, 0], dst_ref=part.at[:, 1], send_sem=ss.at[k], recv_sem=rs.at[k],
            device_id=sib, device_id_type=MESH,
        )
        sent.append(whole)
        return whole

    g_r = send(act.at[:, 0:FBLK], gblk.at[1], right)
    g_l = send(act.at[:, 0:FBLK], gblk.at[2], left)
    swap_b = swap(0)
    swap_a = swap(1)
    w_y = [send(kw.at[part], wbuf.at[y, zh, c, part], to) for to in ys]
    lens_copy.wait()
    row = lax.broadcasted_iota(jnp.int32, (8, T), 0)
    tile = jnp.zeros((8, T), jnp.int32)
    for s in range(8):
        tile = jnp.where(row == s, lens_s[0, s], tile)
    lt[0] = tile
    og_copy.wait()
    scaled = ogv[...].astype(F32) * ratio_of(tile)
    sgs[...] = scaled.astype(BF16)
    sgt[0] = scaled.T.astype(BF16)
    s_copy = send(sgt.at[0], sgt.at[1], sib)
    l_copies = [send(lt.at[0], lt.at[1 + i], to) for i, to in enumerate(group)]

    own_all.wait()
    s_copy.wait_recv()
    heads = jnp.concatenate([sgt[0], sgt[1]], axis=1)

    def block(i):
        return jnp.dot(heads, abuf[i].reshape(2 * T, T), preferred_element_type=F32)

    def block_b(i, _):
        yb[lax.div(i, 8), lax.rem(i, 8)] = block(i)
        return 0

    def block_a(i, _):
        psum[:, i] = block(16 + i).reshape(X, 32, T)
        return 0

    def y_step(buf, up_buf, down_buf, s, before):
        n = buf.shape[-2] // 2
        t = 4 - s
        hi, lo = lax.rem(y + t, Y), lax.rem(y + Y - t, Y)
        if s == 0:
            return [
                send(buf.at[hi, 0:n], up_buf.at[0, 0:n], up),
                send(buf.at[hi, n:2 * n], down_buf.at[0, n:2 * n], down),
            ]
        before[0].wait_recv()
        if s == 1:
            buf[hi, 0:n] += up_buf[0, 0:n]
        else:
            buf[hi] += up_buf[s - 1]
        a = send(buf.at[hi], up_buf.at[s], up)
        before[1].wait_recv()
        if s == 1:
            buf[lo, n:2 * n] += down_buf[0, n:2 * n]
        else:
            buf[lo] += down_buf[s - 1]
        b = send(buf.at[lo], down_buf.at[s], down)
        return [a, b]

    def step_b(k, s, before):
        return y_step(yb.at[k], ybr.at[k], ybl.at[k], s, before)

    def step_a(s, before):
        return y_step(ya, yar, yal, s, before)

    def step_f(s, before):
        return y_step(yf, yfr, yfl, s, before)

    xp, xm, xo = lax.rem(x + 1, X), lax.rem(x + 3, X), lax.rem(x + 2, X)
    swap_b.wait_recv()
    lax.fori_loop(0, 8, block_b, 0, unroll=4)
    b0 = step_b(0, 0, None)
    lax.fori_loop(8, 16, block_b, 0, unroll=4)
    b1 = step_b(1, 0, None)
    swap_a.wait_recv()
    lax.fori_loop(0, 16, block_a, 0, unroll=4)
    r1 = send(psum.at[xo, 0:8], xr.at[0], right)
    l1 = send(psum.at[xo, 8:16], xr.at[1], left)
    blk_copy.wait()
    g_s = [send(gblk.at[0], gblk.at[3], sib)]
    w_copy.wait()
    arrived(w_y)
    w_z = [
        send(wbuf.at[:, zh, c, part], wbuf.at[:, zh, c, part], fore),
        send(wbuf.at[:, zh, c, part], wbuf.at[:, zh, c, part], back),
    ]
    g_r.wait_recv()
    f_r = send(gblk.at[1, 0:64], gblk.at[6, 0:64], right)
    g_l.wait_recv()
    f_l = send(gblk.at[2, 64:128], gblk.at[6, 64:128], left)
    g_s.append(send(gblk.at[1], gblk.at[4], sib))
    g_s.append(send(gblk.at[2], gblk.at[5], sib))

    b0 = step_b(0, 1, b0)
    b1 = step_b(1, 1, b1)
    r2 = send(psum.at[xp, 8:16], xr.at[2], right)
    l2 = send(psum.at[xm, 0:8], xr.at[3], left)

    arrived(l_copies)
    every = lt[...]
    cy[0, 0:8] = jnp.sum(every, axis=0).astype(F32)
    cy[0, 8:16] = jnp.sum((every > 0).astype(jnp.int32), axis=0).astype(F32)
    y_counts = [send(cy.at[0], cy.at[1 + i], to) for i, to in enumerate(ys)]

    mine = pl.ds(pl.multiple_of((2 * x + c) * T, T), T)

    def weigh(s):
        weighted = gblk[s, :, mine].astype(F32) * ratio_of(lt[s])
        wbt[:, s * T:(s + 1) * T] = weighted.T.astype(BF16)

    def rows_of(lo, hi, i):
        return gblk[lo:hi, :, pl.ds(pl.multiple_of(i * T, T), T)].reshape((hi - lo) * T, T)

    def factor_first(i, _):
        yf[i] = jnp.dot(wbt[:, 0:6 * T], rows_of(0, 6, i), preferred_element_type=F32)
        return 0

    def factor_rest(i, _):
        yf[i] += jnp.dot(wbt[:, 6 * T:8 * T], rows_of(6, 8, i), preferred_element_type=F32)
        return 0

    for s in range(3):
        weigh(s)
    for s in range(3):
        g_s[s].wait_recv()
        weigh(3 + s)
    lax.fori_loop(0, Y, factor_first, 0, unroll=4)
    arrived([f_r, f_l])
    g_s.append(send(gblk.at[6], gblk.at[7], sib))
    r1.wait_recv()
    psum[xp, 0:8] += xr[0]
    r3 = send(psum.at[xp, 0:8], xr.at[4], right)
    l1.wait_recv()
    psum[xm, 8:16] += xr[1]
    l3 = send(psum.at[xm, 8:16], xr.at[5], left)
    b0 = step_b(0, 2, b0)
    b1 = step_b(1, 2, b1)
    weigh(6)
    g_s[3].wait_recv()
    weigh(7)
    lax.fori_loop(0, Y, factor_rest, 0, unroll=4)
    f_y = step_f(0, None)
    b0 = step_b(0, 3, b0)
    b1 = step_b(1, 3, b1)
    arrived(y_counts)
    cz[0] = jnp.sum(cy[...], axis=0)
    z_counts = [send(cz.at[0], cz.at[1 + i], to) for i, to in enumerate(zhs)]
    arrived(w_z)
    zp, zm = lax.rem(zh + 1, ZH), lax.rem(zh + 3, ZH)
    w_z = [
        send(wbuf.at[0:4, zm, c, part], wbuf.at[0:4, zm, c, part], fore),
        send(wbuf.at[4:8, zp, c, part], wbuf.at[4:8, zp, c, part], back),
    ]
    l2.wait_recv()
    r3.wait_recv()
    ya[0:4] = (psum[x, 0:8] + xr[3] + xr[4]).reshape(4, 64, T)
    r2.wait_recv()
    l3.wait_recv()
    ya[4:8] = (psum[x, 8:16] + xr[2] + xr[5]).reshape(4, 64, T)
    a_y = step_a(0, None)
    f_y = step_f(1, f_y)
    a_y = step_a(1, a_y)
    b_x = []
    for k, arriving in enumerate([b0, b1]):
        arrived(arriving)
        xb[k] = (yb[k, y] + ybr[k, 3] + ybl[k, 3]).reshape(X, 32, T)
        b_x += [send(xb.at[k, lax.rem(x + 1 + i, X)], xbr.at[k, 1 + i], to) for i, to in enumerate([right, dev(dx=2), left])]
        xbr[k, 0] = xb[k, x]
    arrived(z_counts)
    cl[0] = jnp.sum(cz[...], axis=0)
    l_counts = [send(cl.at[0], cl.at[1 + i], to) for i, to in enumerate(zls)]
    f_y = step_f(2, f_y)

    def quarter(q, lo=0, hi=Y):
        rows = pl.ds(pl.multiple_of(32 * q, 32), 32)
        return wbuf.at[lo:hi, :, c, rows]

    arrived(w_z)
    w_x = [send(quarter(x), quarter(x), right), send(quarter(x), quarter(x), left)]
    w_s = [send(quarter(x), quarter(x), sib)]
    a_y = step_a(2, a_y)
    f_y = step_f(3, f_y)
    a_y = step_a(3, a_y)

    arrived(l_counts)
    total = cl[0] + cl[1] + cl[2]
    valid = jnp.sum(total[0:8], axis=0, keepdims=True)
    seqs = jnp.sum(total[8:16], axis=0, keepdims=True)
    scale_row = valid / seqs
    scale = jnp.max(scale_row)

    arrived(f_y)
    zf[...] = (yf[y] + yfr[3] + yfl[3]).T.reshape(ZH, 32, T)
    f_z = [send(zf.at[lax.rem(zh + 1 + i, ZH)], zfr.at[1 + i], to) for i, to in enumerate(zhs)]
    zfr[0] = zf[zh]
    arrived(b_x)
    zw[0:2] = xbr[:, 0] + xbr[:, 1] + xbr[:, 2] + xbr[:, 3]
    arrived(a_y)
    zw[2:4] = (ya[y] + yar[3] + yal[3]).reshape(2, 32, T)
    w_zs = [send(zw.at[lax.rem(zh + 1 + i, ZH)], zwr.at[1 + i], to) for i, to in enumerate(zhs)]
    zwr[0] = zw[zh]
    arrived(w_x)
    w_x = [send(quarter(xm, 0, 4), quarter(xm, 0, 4), right), send(quarter(xp, 4, 8), quarter(xp, 4, 8), left)]
    w_s += [send(quarter(xm), quarter(xm), sib), send(quarter(xp), quarter(xp), sib)]

    arrived(w_x)
    w_s.append(send(quarter(xo), quarter(xo), sib))

    def product(i):
        out = lax.dot_general(
            sgs[...], wbuf[i].reshape(1024, T), (((1,), (1,)), ((), ())), preferred_element_type=F32
        )
        grad_in[:, i * 1024:(i + 1) * 1024] = (scale * out).astype(BF16)

    arrived(f_z)
    lr[0, 32:64] = zfr[0] + zfr[1] + zfr[2] + zfr[3]
    l_f = [send(lr.at[0, 32:64], lr.at[1 + i, 32:64], to) for i, to in enumerate(zls)]
    arrived(w_zs)
    lr[0, 0:32] = zwr[0] + zwr[1] + zwr[2] + zwr[3]
    l_w = [send(lr.at[0, 0:32], lr.at[1 + i, 0:32], to) for i, to in enumerate(zls)]
    arrived(w_s)
    for i in range(3):
        product(i)
    slot = 2 * x + c
    arrived(l_f)
    finf[...] = (lr[0, 32:64] + lr[1, 32:64] + lr[2, 32:64]).reshape(2, 16, T)
    last = [send(finf.at[1 - c], ff.at[slot], to) for to in other]
    last += [send(finf.at[c], ff.at[slot], to) for to in same]
    ff[slot] = finf[c]
    arrived(l_w)
    done = lr[0, 0:32] + lr[1, 0:32] + lr[2, 0:32]
    finw[...] = done
    last += [send(finw, fw.at[x], to) for to in same]
    fw[x] = done
    for i in range(3, 8):
        product(i)
    arrived(last)
    wgrad[...] = scale * fw[...].reshape(T, T).T
    for g in range(8):
        factor[:, g * T:(g + 1) * T] = ff[g] / seqs
    for copy in sent:
        copy.wait_send()


def shards(activations, out_grad, key_weight, lengths):
    sems = 152
    hbm = pl.BlockSpec(memory_space=pltpu.HBM)
    vmem = pl.BlockSpec(memory_space=pltpu.VMEM)
    return pl.pallas_call(
        kernel,
        out_shape=(
            jax.ShapeDtypeStruct((T, 8192), BF16),
            jax.ShapeDtypeStruct((T, T), F32),
            jax.ShapeDtypeStruct((16, FBLK), F32),
        ),
        in_specs=[hbm, hbm, hbm, hbm],
        out_specs=(vmem, vmem, vmem),
        scratch_shapes=[
            pltpu.VMEM((32, 2, T, T), BF16),
            pltpu.VMEM((2, T, T), BF16),
            pltpu.VMEM((T, T), BF16),
            pltpu.VMEM((X, 16, 32, T), F32),
            pltpu.VMEM((6, 8, 32, T), F32),
            pltpu.VMEM((2, Y, T, T), F32),
            pltpu.VMEM((2, 4, T, T), F32),
            pltpu.VMEM((2, 4, T, T), F32),
            pltpu.VMEM((Y, 64, T), F32),
            pltpu.VMEM((4, 64, T), F32),
            pltpu.VMEM((4, 64, T), F32),
            pltpu.VMEM((Y, T, T), F32),
            pltpu.VMEM((4, T, T), F32),
            pltpu.VMEM((4, T, T), F32),
            pltpu.VMEM((2, X, 32, T), F32),
            pltpu.VMEM((2, X, 32, T), F32),
            pltpu.VMEM((8, T, FBLK), BF16),
            pltpu.VMEM((T, 8 * T), BF16),
            pltpu.VMEM((8, 8, T), jnp.int32),
            pltpu.VMEM((Y, 16, T), F32),
            pltpu.VMEM((ZH, 16, T), F32),
            pltpu.VMEM((ZL, 16, T), F32),
            pltpu.VMEM((Y, ZH, 2, T, T), BF16),
            pltpu.VMEM((ZH, 32, T), F32),
            pltpu.VMEM((ZH, 32, T), F32),
            pltpu.VMEM((ZH, 32, T), F32),
            pltpu.VMEM((ZH, 32, T), F32),
            pltpu.VMEM((ZL, 64, T), F32),
            pltpu.VMEM((32, T), F32),
            pltpu.VMEM((2, 16, T), F32),
            pltpu.VMEM((X, 32, T), F32),
            pltpu.VMEM((8, 16, T), F32),
            pltpu.VMEM((T, T), BF16),
            pltpu.SMEM((1, 8), jnp.int32),
            pltpu.SemaphoreType.DMA((sems,)),
            pltpu.SemaphoreType.DMA((sems,)),
            pltpu.SemaphoreType.DMA((8,)),
        ],
        compiler_params=pltpu.CompilerParams(
            collective_id=0, has_side_effects=True, vmem_limit_bytes=48 * 1024 * 1024
        ),
    )(*[pltpu.with_memory_space_constraint(a, pltpu.HBM) for a in (activations, out_grad, key_weight, lengths)])


def solution(mesh):
    in_specs = (
        P(("rep", "fsdp"), None),
        P(("rep", "fsdp"), None),
        P("fsdp", None),
        P(("rep", "fsdp"), None),
    )
    out_specs = (P(("rep", "fsdp"), None), P("fsdp", None), P("fsdp", None))
    return jax.shard_map(shards, mesh=mesh, in_specs=in_specs, out_specs=out_specs, check_vma=False)
```

```python
import jax
import jax.numpy as jnp
from jax import lax
from jax.experimental import pallas as pl
from jax.experimental.pallas import tpu as pltpu
from jax.sharding import PartitionSpec as P

FBLK = 1024
X, Y, ZH, ZL = 4, 8, 4, 3
T = 128
MESH = pl.DeviceIdType.MESH
F32, BF16 = jnp.float32, jnp.bfloat16


def ratio_of(tile):
    pos = lax.broadcasted_iota(jnp.int32, (T, T), 0)
    end = jnp.zeros((1, T), jnp.int32)
    ratio = jnp.zeros((T, T), F32)
    for s in range(8):
        length = tile[s:s + 1, :]
        start, end = end, end + length
        inverse = 1.0 / jnp.maximum(length, 1).astype(F32)
        ratio = ratio + jnp.where((pos >= start) & (pos < end), inverse, 0.0)
    return ratio


def kernel(
    act, og, kw, lens, grad_in, wgrad, factor,
    abuf, sgt, sgs, psum, xr, yb, ybr, ybl, ya, yar, yal, yf, yfr, yfl, xb, xbr, gblk, wbt, lt, cy, cz, cl,
    wbuf, zw, zwr, zf, zfr, lr, finw, finf, fw, ff, ogv, lens_s, ss, rs, ls,
):
    rep, fs = lax.axis_index("rep"), lax.axis_index("fsdp")
    x, zl = lax.div(rep, ZL), lax.rem(rep, ZL)
    y, zh, c = lax.div(fs, 8), lax.rem(lax.div(fs, 2), ZH), lax.rem(fs, 2)

    def dev(dx=0, dy=0, dzh=0, dzl=0, dc=0):
        c2 = 1 - c if dc else c
        x2, y2, zh2, zl2 = lax.rem(x + dx, X), lax.rem(y + dy, Y), lax.rem(zh + dzh, ZH), lax.rem(zl + dzl, ZL)
        return (x2 * ZL + zl2, y2 * 8 + zh2 * 2 + c2)

    sib, right, left = dev(dc=1), dev(dx=1), dev(dx=3)
    up, down = dev(dy=1), dev(dy=7)
    fore, back = dev(dzh=1), dev(dzh=3)
    group = [right, left, sib, dev(dx=1, dc=1), dev(dx=3, dc=1), dev(dx=2), dev(dx=2, dc=1)]
    same, other = [group[0], group[1], group[5]], [group[2], group[3], group[4], group[6]]
    ys = [dev(dy=d) for d in range(1, Y)]
    zhs = [dev(dzh=d) for d in range(1, ZH)]
    zls = [dev(dzl=d) for d in range(1, ZL)]
    count = [0]
    sent = []

    def send(src, dst, to):
        k = count[0]
        count[0] += 1
        copy = pltpu.make_async_remote_copy(
            src_ref=src, dst_ref=dst, send_sem=ss.at[k], recv_sem=rs.at[k],
            device_id=to, device_id_type=MESH,
        )
        copy.start()
        sent.append(copy)
        return copy

    def arrived(copies):
        for copy in copies:
            copy.wait_recv()

    lens_copy = pltpu.make_async_copy(lens, lens_s, ls.at[4])
    lens_copy.start()
    og_copy = pltpu.make_async_copy(og, ogv, ls.at[1])
    og_copy.start()

    barrier = pltpu.get_barrier_semaphore()
    peers = group + ys + zhs + zls
    for peer in peers:
        pl.semaphore_signal(barrier, inc=1, device_id=peer, device_id_type=MESH)

    def cols(i, half, core):
        if half == 0:
            b = lax.rem(i, 8) * 8 + lax.div(i, 8) * 2 + core
        else:
            b = lax.div(i, 2) * 8 + 4 + lax.rem(i, 2) * 2 + core
        return act.at[:, pl.ds(pl.multiple_of(b * T, T), T)]

    for half in range(2):
        def start_own(i, _, half=half):
            pltpu.make_async_copy(cols(i, half, c), abuf.at[16 * half + i, 0], ls.at[0]).start()
            return 0

        lax.fori_loop(0, 16, start_own, 0)
    own_all = pltpu.make_async_copy(abuf.at[:, 0], abuf.at[:, 0], ls.at[0])
    blk_copy = pltpu.make_async_copy(act.at[:, 0:FBLK], gblk.at[0], ls.at[3])
    blk_copy.start()
    part = pl.ds(pl.multiple_of(32 * x, 32), 32)
    w_copy = pltpu.make_async_copy(kw.at[part], wbuf.at[y, zh, c, part], ls.at[2])
    w_copy.start()

    pl.semaphore_wait(barrier, len(peers))

    act_k = count[0]
    count[0] += 2

    def swap(half):
        k = act_k + half

        def start(i, _):
            pltpu.make_async_remote_copy(
                src_ref=cols(i, half, 1 - c), dst_ref=abuf.at[16 * half + i, 1], send_sem=ss.at[k], recv_sem=rs.at[k],
                device_id=sib, device_id_type=MESH,
            ).start()
            return 0

        lax.fori_loop(0, 16, start, 0)
        part = abuf.at[16 * half:16 * half + 16]
        whole = pltpu.make_async_remote_copy(
            src_ref=part.at[:, 0], dst_ref=part.at[:, 1], send_sem=ss.at[k], recv_sem=rs.at[k],
            device_id=sib, device_id_type=MESH,
        )
        sent.append(whole)
        return whole

    g_r = send(act.at[:, 0:FBLK], gblk.at[1], right)
    g_l = send(act.at[:, 0:FBLK], gblk.at[2], left)
    swap_b = swap(0)
    swap_a = swap(1)
    w_y = [send(kw.at[part], wbuf.at[y, zh, c, part], to) for to in ys]
    lens_copy.wait()
    row = lax.broadcasted_iota(jnp.int32, (8, T), 0)
    tile = jnp.zeros((8, T), jnp.int32)
    for s in range(8):
        tile = jnp.where(row == s, lens_s[0, s], tile)
    lt[0] = tile
    og_copy.wait()
    scaled = ogv[...].astype(F32) * ratio_of(tile)
    sgs[...] = scaled.astype(BF16)
    sgt[0] = scaled.T.astype(BF16)
    s_copy = send(sgt.at[0], sgt.at[1], sib)
    l_copies = [send(lt.at[0], lt.at[1 + i], to) for i, to in enumerate(group)]

    own_all.wait()
    s_copy.wait_recv()
    heads = jnp.concatenate([sgt[0], sgt[1]], axis=1)

    def block(i):
        return jnp.dot(heads, abuf[i].reshape(2 * T, T), preferred_element_type=F32)

    def block_b(i, _):
        yb[lax.div(i, 8), lax.rem(i, 8)] = block(i)
        return 0

    def block_a(i, _):
        psum[:, i] = block(16 + i).reshape(X, 32, T)
        return 0

    def y_step(buf, up_buf, down_buf, s, before):
        n = buf.shape[-2] // 2
        t = 4 - s
        hi, lo = lax.rem(y + t, Y), lax.rem(y + Y - t, Y)
        if s == 0:
            return [
                send(buf.at[hi, 0:n], up_buf.at[0, 0:n], up),
                send(buf.at[hi, n:2 * n], down_buf.at[0, n:2 * n], down),
            ]
        before[0].wait_recv()
        if s == 1:
            buf[hi, 0:n] += up_buf[0, 0:n]
        else:
            buf[hi] += up_buf[s - 1]
        a = send(buf.at[hi], up_buf.at[s], up)
        before[1].wait_recv()
        if s == 1:
            buf[lo, n:2 * n] += down_buf[0, n:2 * n]
        else:
            buf[lo] += down_buf[s - 1]
        b = send(buf.at[lo], down_buf.at[s], down)
        return [a, b]

    def step_b(k, s, before):
        return y_step(yb.at[k], ybr.at[k], ybl.at[k], s, before)

    def step_a(s, before):
        return y_step(ya, yar, yal, s, before)

    def step_f(s, before):
        return y_step(yf, yfr, yfl, s, before)

    xp, xm, xo = lax.rem(x + 1, X), lax.rem(x + 3, X), lax.rem(x + 2, X)
    swap_b.wait_recv()
    lax.fori_loop(0, 8, block_b, 0, unroll=4)
    b0 = step_b(0, 0, None)
    lax.fori_loop(8, 16, block_b, 0, unroll=4)
    b1 = step_b(1, 0, None)
    swap_a.wait_recv()
    lax.fori_loop(0, 16, block_a, 0, unroll=4)
    r1 = send(psum.at[xo, 0:8], xr.at[0], right)
    l1 = send(psum.at[xo, 8:16], xr.at[1], left)
    blk_copy.wait()
    g_s = [send(gblk.at[0], gblk.at[3], sib)]
    w_copy.wait()
    arrived(w_y)
    w_z = [
        send(wbuf.at[:, zh, c, part], wbuf.at[:, zh, c, part], fore),
        send(wbuf.at[:, zh, c, part], wbuf.at[:, zh, c, part], back),
    ]
    g_r.wait_recv()
    f_r = send(gblk.at[1, 0:64], gblk.at[6, 0:64], right)
    g_l.wait_recv()
    f_l = send(gblk.at[2, 64:128], gblk.at[6, 64:128], left)
    g_s.append(send(gblk.at[1], gblk.at[4], sib))
    g_s.append(send(gblk.at[2], gblk.at[5], sib))

    b0 = step_b(0, 1, b0)
    b1 = step_b(1, 1, b1)
    r2 = send(psum.at[xp, 8:16], xr.at[2], right)
    l2 = send(psum.at[xm, 0:8], xr.at[3], left)

    arrived(l_copies)
    every = lt[...]
    cy[0, 0:8] = jnp.sum(every, axis=0).astype(F32)
    cy[0, 8:16] = jnp.sum((every > 0).astype(jnp.int32), axis=0).astype(F32)
    y_counts = [send(cy.at[0], cy.at[1 + i], to) for i, to in enumerate(ys)]

    mine = pl.ds(pl.multiple_of((2 * x + c) * T, T), T)

    def weigh(s):
        weighted = gblk[s, :, mine].astype(F32) * ratio_of(lt[s])
        wbt[:, s * T:(s + 1) * T] = weighted.T.astype(BF16)

    def rows_of(lo, hi, i):
        return gblk[lo:hi, :, pl.ds(pl.multiple_of(i * T, T), T)].reshape((hi - lo) * T, T)

    def factor_first(i, _):
        yf[i] = jnp.dot(wbt[:, 0:6 * T], rows_of(0, 6, i), preferred_element_type=F32)
        return 0

    def factor_rest(i, _):
        yf[i] += jnp.dot(wbt[:, 6 * T:8 * T], rows_of(6, 8, i), preferred_element_type=F32)
        return 0

    for s in range(3):
        weigh(s)
    for s in range(3):
        g_s[s].wait_recv()
        weigh(3 + s)
    lax.fori_loop(0, Y, factor_first, 0, unroll=4)
    arrived([f_r, f_l])
    g_s.append(send(gblk.at[6], gblk.at[7], sib))
    r1.wait_recv()
    psum[xp, 0:8] += xr[0]
    r3 = send(psum.at[xp, 0:8], xr.at[4], right)
    l1.wait_recv()
    psum[xm, 8:16] += xr[1]
    l3 = send(psum.at[xm, 8:16], xr.at[5], left)
    b0 = step_b(0, 2, b0)
    b1 = step_b(1, 2, b1)
    weigh(6)
    g_s[3].wait_recv()
    weigh(7)
    lax.fori_loop(0, Y, factor_rest, 0, unroll=4)
    f_y = step_f(0, None)
    b0 = step_b(0, 3, b0)
    b1 = step_b(1, 3, b1)
    arrived(y_counts)
    cz[0] = jnp.sum(cy[...], axis=0)
    z_counts = [send(cz.at[0], cz.at[1 + i], to) for i, to in enumerate(zhs)]
    arrived(w_z)
    zp, zm = lax.rem(zh + 1, ZH), lax.rem(zh + 3, ZH)
    w_z = [
        send(wbuf.at[0:4, zm, c, part], wbuf.at[0:4, zm, c, part], fore),
        send(wbuf.at[4:8, zp, c, part], wbuf.at[4:8, zp, c, part], back),
    ]
    l2.wait_recv()
    r3.wait_recv()
    ya[0:4] = (psum[x, 0:8] + xr[3] + xr[4]).reshape(4, 64, T)
    r2.wait_recv()
    l3.wait_recv()
    ya[4:8] = (psum[x, 8:16] + xr[2] + xr[5]).reshape(4, 64, T)
    a_y = step_a(0, None)
    f_y = step_f(1, f_y)
    a_y = step_a(1, a_y)
    b_x = []
    for k, arriving in enumerate([b0, b1]):
        arrived(arriving)
        xb[k] = (yb[k, y] + ybr[k, 3] + ybl[k, 3]).reshape(X, 32, T)
        b_x += [send(xb.at[k, lax.rem(x + 1 + i, X)], xbr.at[k, 1 + i], to) for i, to in enumerate([right, dev(dx=2), left])]
        xbr[k, 0] = xb[k, x]
    arrived(z_counts)
    cl[0] = jnp.sum(cz[...], axis=0)
    l_counts = [send(cl.at[0], cl.at[1 + i], to) for i, to in enumerate(zls)]
    f_y = step_f(2, f_y)

    def quarter(q, lo=0, hi=Y):
        rows = pl.ds(pl.multiple_of(32 * q, 32), 32)
        return wbuf.at[lo:hi, :, c, rows]

    arrived(w_z)
    w_x = [send(quarter(x), quarter(x), right), send(quarter(x), quarter(x), left)]
    w_s = [send(quarter(x), quarter(x), sib)]
    a_y = step_a(2, a_y)
    f_y = step_f(3, f_y)
    a_y = step_a(3, a_y)

    arrived(l_counts)
    total = cl[0] + cl[1] + cl[2]
    valid = jnp.sum(total[0:8], axis=0, keepdims=True)
    seqs = jnp.sum(total[8:16], axis=0, keepdims=True)
    scale_row = valid / seqs
    scale = jnp.max(scale_row)

    arrived(f_y)
    zf[...] = (yf[y] + yfr[3] + yfl[3]).T.reshape(ZH, 32, T)
    f_z = [send(zf.at[lax.rem(zh + 1 + i, ZH)], zfr.at[1 + i], to) for i, to in enumerate(zhs)]
    zfr[0] = zf[zh]
    arrived(b_x)
    zw[0:2] = xbr[:, 0] + xbr[:, 1] + xbr[:, 2] + xbr[:, 3]
    arrived(a_y)
    zw[2:4] = (ya[y] + yar[3] + yal[3]).reshape(2, 32, T)
    w_zs = [send(zw.at[lax.rem(zh + 1 + i, ZH)], zwr.at[1 + i], to) for i, to in enumerate(zhs)]
    zwr[0] = zw[zh]
    arrived(w_x)
    w_x = [send(quarter(xm, 0, 4), quarter(xm, 0, 4), right), send(quarter(xp, 4, 8), quarter(xp, 4, 8), left)]
    w_s += [send(quarter(xm), quarter(xm), sib), send(quarter(xp), quarter(xp), sib)]

    arrived(w_x)
    w_s.append(send(quarter(xo), quarter(xo), sib))

    def product(i):
        out = lax.dot_general(
            sgs[...], wbuf[i].reshape(1024, T), (((1,), (1,)), ((), ())), preferred_element_type=F32
        )
        grad_in[:, i * 1024:(i + 1) * 1024] = (scale * out).astype(BF16)

    arrived(f_z)
    lr[0, 32:64] = zfr[0] + zfr[1] + zfr[2] + zfr[3]
    l_f = [send(lr.at[0, 32:64], lr.at[1 + i, 32:64], to) for i, to in enumerate(zls)]
    arrived(w_zs)
    lr[0, 0:32] = zwr[0] + zwr[1] + zwr[2] + zwr[3]
    l_w = [send(lr.at[0, 0:32], lr.at[1 + i, 0:32], to) for i, to in enumerate(zls)]
    arrived(w_s)
    for i in range(3):
        product(i)
    slot = 2 * x + c
    arrived(l_f)
    finf[...] = (lr[0, 32:64] + lr[1, 32:64] + lr[2, 32:64]).reshape(2, 16, T)
    last = [send(finf.at[1 - c], ff.at[slot], to) for to in other]
    last += [send(finf.at[c], ff.at[slot], to) for to in same]
    ff[slot] = finf[c]
    arrived(l_w)
    done = lr[0, 0:32] + lr[1, 0:32] + lr[2, 0:32]
    finw[...] = done
    last += [send(finw, fw.at[x], to) for to in same]
    fw[x] = done
    for i in range(3, 8):
        product(i)
    arrived(last[:7])
    for g in range(8):
        factor[:, g * T:(g + 1) * T] = ff[g] / seqs
    arrived(last[7:])
    wgrad[...] = scale * fw[...].reshape(T, T).T
    for copy in sent:
        copy.wait_send()


def shards(activations, out_grad, key_weight, lengths):
    sems = 152
    hbm = pl.BlockSpec(memory_space=pltpu.HBM)
    vmem = pl.BlockSpec(memory_space=pltpu.VMEM)
    return pl.pallas_call(
        kernel,
        out_shape=(
            jax.ShapeDtypeStruct((T, 8192), BF16),
            jax.ShapeDtypeStruct((T, T), F32),
            jax.ShapeDtypeStruct((16, FBLK), F32),
        ),
        in_specs=[hbm, hbm, hbm, hbm],
        out_specs=(vmem, vmem, vmem),
        scratch_shapes=[
            pltpu.VMEM((32, 2, T, T), BF16),
            pltpu.VMEM((2, T, T), BF16),
            pltpu.VMEM((T, T), BF16),
            pltpu.VMEM((X, 16, 32, T), F32),
            pltpu.VMEM((6, 8, 32, T), F32),
            pltpu.VMEM((2, Y, T, T), F32),
            pltpu.VMEM((2, 4, T, T), F32),
            pltpu.VMEM((2, 4, T, T), F32),
            pltpu.VMEM((Y, 64, T), F32),
            pltpu.VMEM((4, 64, T), F32),
            pltpu.VMEM((4, 64, T), F32),
            pltpu.VMEM((Y, T, T), F32),
            pltpu.VMEM((4, T, T), F32),
            pltpu.VMEM((4, T, T), F32),
            pltpu.VMEM((2, X, 32, T), F32),
            pltpu.VMEM((2, X, 32, T), F32),
            pltpu.VMEM((8, T, FBLK), BF16),
            pltpu.VMEM((T, 8 * T), BF16),
            pltpu.VMEM((8, 8, T), jnp.int32),
            pltpu.VMEM((Y, 16, T), F32),
            pltpu.VMEM((ZH, 16, T), F32),
            pltpu.VMEM((ZL, 16, T), F32),
            pltpu.VMEM((Y, ZH, 2, T, T), BF16),
            pltpu.VMEM((ZH, 32, T), F32),
            pltpu.VMEM((ZH, 32, T), F32),
            pltpu.VMEM((ZH, 32, T), F32),
            pltpu.VMEM((ZH, 32, T), F32),
            pltpu.VMEM((ZL, 64, T), F32),
            pltpu.VMEM((32, T), F32),
            pltpu.VMEM((2, 16, T), F32),
            pltpu.VMEM((X, 32, T), F32),
            pltpu.VMEM((8, 16, T), F32),
            pltpu.VMEM((T, T), BF16),
            pltpu.SMEM((1, 8), jnp.int32),
            pltpu.SemaphoreType.DMA((sems,)),
            pltpu.SemaphoreType.DMA((sems,)),
            pltpu.SemaphoreType.DMA((8,)),
        ],
        compiler_params=pltpu.CompilerParams(
            collective_id=0, has_side_effects=True, vmem_limit_bytes=48 * 1024 * 1024
        ),
    )(*[pltpu.with_memory_space_constraint(a, pltpu.HBM) for a in (activations, out_grad, key_weight, lengths)])


def solution(mesh):
    in_specs = (
        P(("rep", "fsdp"), None),
        P(("rep", "fsdp"), None),
        P("fsdp", None),
        P(("rep", "fsdp"), None),
    )
    out_specs = (P(("rep", "fsdp"), None), P("fsdp", None), P("fsdp", None))
    return jax.shard_map(shards, mesh=mesh, in_specs=in_specs, out_specs=out_specs, check_vma=False)
```
